128 devices in a mesh: ctx: 16 (over z_hi, x, core), tp: 8 (over y, z_lo).
Axes of the slice: x: 4, y: 4, z: 4 (z_hi: 2, z_lo: 2; z = z_hi * 2 + z_lo), core: 2. Of those that a mesh axis runs over, the one named last changes fastest.
Arguments:
- outer_gate: bfloat16 [8192, 8192], P('ctx', 'tp'), may hold values from -6 to 6
- inner_gate: bfloat16 [8192, 8192], P('ctx', 'tp'), may hold values from -6 to 6
- signal: bfloat16 [8192, 8192], P('ctx', 'tp'), may hold values from -6 to 6
- filter_taps: float32 [8192, 8192], P('ctx', 'tp'), may hold values from -0.0625 to 0.0625
- skip_gain: float32 [8192], P('tp'), may hold values from 0.25 to 2
- out_weight: bfloat16 [8192, 8192], P('tp'), may hold values from -0.0625 to 0.0625
Outputs:
- projected: bfloat16 [8192, 8192], P('ctx', 'tp')
The draws below stay inside these ranges and needn't reach their ends.
All inputs are finite; a program needn't handle non-finite values.
Results may differ from the reference program's by a relative error of at most 0.0049.
Values sent between devices are 32-bit elements; how exact they have to be, the bound alone decides.
A program may use at most 128 MiB of HBM per device.

```python
import jax
import jax.numpy as jnp
from jax import lax

D = 8192
TOKENS = 8192


def block_levels(rng, extent, cuts, smallest, high):
    factor_of, own = 1.0, jax.random.fold_in(rng, 6)
    for dim, blocks in cuts:
        steps = jnp.exp(jax.random.uniform(jax.random.fold_in(own, dim), (blocks,), jnp.float32, smallest / len(cuts), high / len(cuts)))
        factor_of = factor_of * jnp.repeat(steps, extent[dim] // blocks).reshape([-1 if axis == dim else 1 for axis in range(len(extent))])
    return factor_of


def scatter_about(stream_key, shape, scale, bound, split=(), held_as=jnp.bfloat16):
    level = block_levels(stream_key, shape, split, -0.22, 0.18) if split else 1.0
    values = jax.random.normal(stream_key, shape, jnp.float32) * scale * level
    return jnp.minimum(jnp.maximum(values, -bound), bound).astype(held_as)


def setup_inputs(seed: int = 0) -> dict:
    arg_keys = jax.random.split(jax.random.key(seed), 7)
    outer_gate = scatter_about(arg_keys[0], (TOKENS, D), 1.0, 6.0, ((0, 16), (1, 8)))
    inner_gate = scatter_about(arg_keys[1], (TOKENS, D), 1.0, 6.0, ((0, 16), (1, 8)))
    signal = scatter_about(arg_keys[2], (TOKENS, D), 1.0, 6.0, ((0, 16), (1, 8)))
    filter_taps = scatter_about(arg_keys[3], (TOKENS, D), TOKENS ** -0.5, 0.0625, ((0, 16), (1, 8)), jnp.float32)
    skip_gain = jnp.clip(0.25 + 1.75 * jax.random.uniform(arg_keys[4], (D,), jnp.float32) ** block_levels(arg_keys[4], (D,), ((0, 8),), -0.2, 0.2), 0.25, 2.0)
    out_weight = scatter_about(arg_keys[5], (D, D), D ** -0.5, 0.0625, ((0, 8),))
    return dict(outer_gate=outer_gate, inner_gate=inner_gate, signal=signal, filter_taps=filter_taps, skip_gain=skip_gain, out_weight=out_weight)


def circular_block(pair):
    values, taps = pair
    spectrum = jnp.fft.fft(values, axis=0) * jnp.fft.fft(taps, axis=0)
    return jnp.real(jnp.fft.ifft(spectrum, axis=0)).astype(values.dtype)


def reference(outer_gate, inner_gate, signal, filter_taps, skip_gain, out_weight):
    gated = inner_gate.astype(jnp.float32) * signal.astype(jnp.float32)
    group = min(D, 512)
    count = D // group
    blocks = gated.reshape(TOKENS, count, group).transpose(1, 0, 2)
    taps = filter_taps.reshape(TOKENS, count, group).transpose(1, 0, 2)
    conv = lax.map(circular_block, (blocks, taps))
    conv = conv.transpose(1, 0, 2).reshape(TOKENS, D)
    mixed = (outer_gate.astype(jnp.float32) * (conv + skip_gain * gated)).astype(jnp.bfloat16)
    return jnp.dot(mixed, out_weight, preferred_element_type=jnp.float32).astype(jnp.bfloat16)
```

```python
import functools
import math

import jax
import jax.numpy as jnp
import numpy as np
from jax import lax
from jax.experimental import pallas as pl
from jax.experimental.pallas import tpu as pltpu
from jax.sharding import PartitionSpec as P

MESH = pl.DeviceIdType.MESH
F32 = jnp.float32
BF16 = jnp.bfloat16

ORDER = ((2, 1), (2, -1), (1, 1), (-1, -1), (1, -1), (-1, 1), (0, 1), (0, -1))
ROWS_A = 224


def split(value):
    high = value.astype(BF16)
    low = (value - high.astype(F32)).astype(BF16)
    return high, low


def split_np(value):
    value = np.asarray(value, np.float64)
    high = value.astype(BF16)
    low = (value - high.astype(np.float64)).astype(BF16)
    return np.stack([high, low])


def tables():
    n1 = np.arange(64)[None, :]
    k1 = np.arange(32)[:, None]
    cos = np.cos(2 * np.pi * (n1 * k1 % 64) / 64)
    sin = np.sin(2 * np.pi * (n1 * k1 % 64) / 64)
    ahead = np.stack([cos, -sin], axis=1)
    ahead[0, 1] = (-1.0) ** np.arange(64)
    ahead = ahead.reshape(64, 64)
    back = np.stack([2 * cos, -2 * sin], axis=1)
    back[0, 0] = 1.0
    back[0, 1] = (-1.0) ** np.arange(64)
    back = back.reshape(64, 64).T / 8192
    eye = np.eye(8)
    n2 = np.arange(128)
    angle = 2 * np.pi * (n2[:, None] * n2[None, :] % 128) / 128
    c, s = np.cos(angle), np.sin(angle)
    fwd = np.block([[c, s], [-s, c]])
    inv = np.block([[c, -s], [s, c]])
    turn = 2 * np.pi * (n2[:, None] * np.arange(33)[None, :]) / 8192
    twist = np.zeros((128, 128))
    twist[:, :33] = np.cos(turn)
    twist[:, 64:97] = np.sin(turn)
    return (
        split_np(np.kron(ahead, eye)),
        split_np(np.kron(back, eye)),
        split_np(fwd),
        split_np(inv),
        twist.astype(np.float32),
    )


def dot3(matrix_ref, value):
    high, low = split(value)
    big, small = matrix_ref[0], matrix_ref[1]
    total = jnp.dot(big, low, preferred_element_type=F32)
    total += jnp.dot(small, high, preferred_element_type=F32)
    return total + jnp.dot(big, high, preferred_element_type=F32)


def here():
    ctx, tp = lax.axis_index("ctx"), lax.axis_index("tp")
    return ctx, tp


def conv_kernel(
    inner_ref, signal_ref, taps_ref, skip_ref, outer_hbm, ahead_hbm, back_hbm, fwd_hbm, inv_hbm, twist_hbm,
    mixed_ref,
    send, recv, spec, prod, result, home,
    outer_ref, ahead_ref, back_ref, fwd_ref, inv_ref, twist_ref,
    load_sem, out_send, out_recv, back_send, back_recv,
):
    ctx, tp = here()
    z_hi, x, core, z_lo = ctx // 8, (ctx // 2) % 4, ctx % 2, tp % 2
    z = 2 * z_hi + z_lo
    partner_tp = tp + 1 - 2 * z_lo
    sign = 1 - 2 * core

    loads = []
    for i, (src, dst) in enumerate(
        (
            (ahead_hbm, ahead_ref), (fwd_hbm, fwd_ref), (inv_hbm, inv_ref),
            (back_hbm, back_ref), (twist_hbm, twist_ref), (outer_hbm, outer_ref),
        )
    ):
        copy = pltpu.make_async_copy(src, dst, load_sem.at[i])
        copy.start()
        loads.append(copy)

    quads = []
    for dx, dz in ORDER:
        to_z = (z + dz * sign + 4) % 4
        quads.append((to_z // 2) * 4 + (x + dx * sign + 4) % 4)

    barrier = pltpu.get_barrier_semaphore()
    for q in quads:
        for k in (0, 1):
            pl.semaphore_signal(barrier, inc=1, device_id=(2 * q + k, partner_tp), device_id_type=MESH)

    lane = lax.broadcasted_iota(jnp.int32, (128, 128), 1)
    first = lane < 64
    row0 = lax.broadcasted_iota(jnp.int32, (128, 128), 0)
    sends = []
    for step, q in enumerate(quads):
        columns = pl.ds(pl.multiple_of(q * 128, 128), 128)
        skip = skip_ref[:, columns]

        def pack(i, carry, columns=columns, skip=skip, q=q):
            rows = pl.ds(pl.multiple_of(i * 128, 128), 128)
            gated = inner_ref[rows, columns].astype(F32) * signal_ref[rows, columns].astype(F32)
            tap0 = jnp.logical_and(row0 + i * 128 + ctx * 512 == 0, True)
            taps = taps_ref[rows, columns] + jnp.where(tap0, skip, 0.0)
            send[2 * q, rows, :] = jnp.where(first, gated, pltpu.roll(taps, 64, 1))
            send[2 * q + 1, rows, :] = jnp.where(first, pltpu.roll(gated, 64, 1), taps)
            return carry

        lax.fori_loop(0, 4, pack, 0)
        if step == 0:
            pl.semaphore_wait(barrier, 16)
        for dk in (0, 1):
            k = (core + dk) % 2
            copy = pltpu.make_async_remote_copy(
                send.at[2 * q + k], recv.at[ctx],
                out_send.at[2 * step + dk], out_recv.at[2 * step + dk],
                device_id=(2 * q + k, partner_tp), device_id_type=MESH,
            )
            copy.start()
            sends.append(copy)
    for copy in loads:
        copy.wait()
    for copy in sends:
        copy.wait_recv()

    first8 = lax.broadcasted_iota(jnp.int32, (8, 128), 1) < 64

    def stage_one(a, carry):
        near = recv.at[:, :, :]
        parts = []
        for half in (0, 1):
            start = pl.multiple_of(half * 64 + a * 8, 8)
            parts.append(
                jnp.concatenate(
                    [
                        recv[s, pl.ds(pl.multiple_of(j * 128 + start, 8), 8), :]
                        for s in range(16)
                        for j in range(4)
                    ],
                    axis=0,
                )
            )
        out = dot3(ahead_ref, jnp.concatenate(parts, axis=1))
        for half in (0, 1):
            rows = pl.ds(pl.multiple_of(half * 64 + a * 8, 8), 8)
            twist = twist_ref[rows, :]
            for k1 in range(33):
                if k1 == 0:
                    spec[0, 0, rows, :] = out[0:8, half * 128 : half * 128 + 128]
                    spec[0, 1, rows, :] = jnp.zeros((8, 128), F32)
                    continue
                cos, sin = twist[:, k1 : k1 + 1], twist[:, 64 + k1 : 65 + k1]
                if k1 == 32:
                    real = out[8:16, half * 128 : half * 128 + 128]
                    spec[32, 0, rows, :] = real * cos
                    spec[32, 1, rows, :] = -(real * sin)
                    continue
                real = out[16 * k1 : 16 * k1 + 8, half * 128 : half * 128 + 128]
                imag = out[16 * k1 + 8 : 16 * k1 + 16, half * 128 : half * 128 + 128]
                spec[k1, 0, rows, :] = real * cos + imag * sin
                spec[k1, 1, rows, :] = imag * cos - real * sin
        return carry

    lax.fori_loop(0, 8, stage_one, 0)

    def product(out, j):
        real, imag = out[:128, 128 * j : 128 * j + 128], out[128:, 128 * j : 128 * j + 128]
        real2, imag2 = pltpu.roll(real, 64, 1), pltpu.roll(imag, 64, 1)
        return jnp.concatenate([real * real2 - imag * imag2, real * imag2 + imag * real2], axis=0)

    first256 = lax.broadcasted_iota(jnp.int32, (256, 128), 1) < 64

    def stage_two(i, carry):
        value = jnp.concatenate([spec[4 * i + j].reshape(256, 128) for j in range(4)], axis=1)
        out = dot3(fwd_ref, value)
        pairs = [
            jnp.where(first256, product(out, 2 * j), product(out, 2 * j + 1)) for j in range(2)
        ]
        out = dot3(inv_ref, jnp.concatenate(pairs, axis=1))
        for j in range(2):
            prod[2 * i + j] = out[:, 128 * j : 128 * j + 128].reshape(2, 128, 128)
        return carry

    lax.fori_loop(0, 8, stage_two, 0)
    out = dot3(fwd_ref, spec[32].reshape(256, 128))
    prod[16] = dot3(inv_ref, product(out, 0)).reshape(2, 128, 128)

    def stage_three(a2, carry):
        sides = []
        for side in (0, 1):
            a = 2 * a2 + side
            low = pl.ds(pl.multiple_of(a * 8, 8), 8)
            high = pl.ds(pl.multiple_of(64 + a * 8, 8), 8)
            near, far = twist_ref[low, :], twist_ref[high, :]

            def turn(k1):
                cos = jnp.where(first8, near[:, k1 : k1 + 1], far[:, k1 : k1 + 1])
                sin = jnp.where(first8, near[:, 64 + k1 : 65 + k1], far[:, 64 + k1 : 65 + k1])
                return cos, sin

            pieces = []
            for pair in range(16):
                here_re, here_im = prod[pair, 0, low, :], prod[pair, 1, low, :]
                next_re, next_im = prod[pair, 0, high, :], prod[pair, 1, high, :]
                for odd in (0, 1):
                    k1 = 2 * pair + odd
                    if odd:
                        real = jnp.where(first8, pltpu.roll(here_re, 64, 1), next_re)
                        imag = jnp.where(first8, pltpu.roll(here_im, 64, 1), next_im)
                    else:
                        real = jnp.where(first8, here_re, pltpu.roll(next_re, 64, 1))
                        imag = jnp.where(first8, here_im, pltpu.roll(next_im, 64, 1))
                    if k1 == 0:
                        pieces.append(real)
                        real = jnp.where(first8, prod[16, 0, low, :], prod[16, 0, high, :])
                        imag = jnp.where(first8, prod[16, 1, low, :], prod[16, 1, high, :])
                        cos, sin = turn(32)
                        pieces.append(real * cos - imag * sin)
                        continue
                    cos, sin = turn(k1)
                    pieces.append(real * cos - imag * sin)
                    pieces.append(real * sin + imag * cos)
            sides.append(jnp.concatenate(pieces, axis=0))
        out = dot3(back_ref, jnp.concatenate(sides, axis=1))
        for side in (0, 1):
            rows = pl.ds(pl.multiple_of((2 * a2 + side) * 8, 8), 8)
            result[:, rows, :] = out[:, 128 * side : 128 * side + 128].reshape(64, 8, 128)
        return carry

    lax.fori_loop(0, 4, stage_three, 0)

    returns = []
    for step, q in enumerate(quads):
        for dk in (0, 1):
            other = 2 * q + (core + dk) % 2
            copy = pltpu.make_async_remote_copy(
                result.at[pl.ds(4 * other, 4)], home.at[ctx],
                back_send.at[2 * step + dk], back_recv.at[2 * step + dk],
                device_id=(other, partner_tp), device_id_type=MESH,
            )
            copy.start()
            returns.append(copy)
    for copy in returns:
        copy.wait_recv()
    first64 = lax.broadcasted_iota(jnp.int32, (64, 128), 1) < 64
    for q in range(8):

        def gate(j, carry, q=q):
            even, odd = home[2 * q, j], home[2 * q + 1, j]
            base = pl.multiple_of(j * 128, 128)
            for rows, conv in (
                (pl.ds(base, 64), jnp.where(first64, even, pltpu.roll(odd, 64, 1))),
                (pl.ds(base + 64, 64), jnp.where(first64, pltpu.roll(even, 64, 1), odd)),
            ):
                gated = outer_ref[rows, 128 * q : 128 * q + 128].astype(F32) * conv
                mixed_ref[rows, 128 * q : 128 * q + 128] = gated.astype(BF16)
            return carry

        lax.fori_loop(0, 4, gate, 0)
    for copy in sends + returns:
        copy.wait_send()


def convolve(outer, inner, signal, taps, skip):
    ahead, back, fwd, inv, twist = tables()
    vmem = pl.BlockSpec(memory_space=pltpu.VMEM)
    hbm = pl.BlockSpec(memory_space=pl.ANY)
    dma = pltpu.SemaphoreType.DMA
    return pl.pallas_call(
        conv_kernel,
        name="convolve",
        out_shape=jax.ShapeDtypeStruct((512, 1024), BF16),
        in_specs=[vmem] * 4 + [hbm] * 6,
        out_specs=vmem,
        scratch_shapes=[
            pltpu.VMEM((16, 512, 128), F32),
            pltpu.VMEM((16, 512, 128), F32),
            pltpu.VMEM((33, 2, 128, 128), F32),
            pltpu.VMEM((17, 2, 128, 128), F32),
            pltpu.VMEM((64, 64, 128), F32),
            pltpu.VMEM((16, 4, 64, 128), F32),
            pltpu.VMEM((512, 1024), BF16),
            pltpu.VMEM((2, 512, 512), BF16),
            pltpu.VMEM((2, 512, 512), BF16),
            pltpu.VMEM((2, 256, 256), BF16),
            pltpu.VMEM((2, 256, 256), BF16),
            pltpu.VMEM((128, 128), F32),
            dma((6,)), dma((16,)), dma((16,)), dma((16,)), dma((16,)),
        ],
        compiler_params=pltpu.CompilerParams(
            collective_id=0, has_side_effects=True, vmem_limit_bytes=56 << 20
        ),
    )(inner, signal, taps, skip.reshape(1, -1), outer, ahead, back, fwd, inv, twist)


def project_kernel(
    mixed_ref, weight_hbm, out_ref,
    weight, part, in_b, in_a, in_za, in_zb,
    load_sem, yb_send, yb_recv, ya_send, ya_recv, za_send, za_recv, zb_send, zb_recv,
):
    ctx, tp = here()
    y, z_lo = tp // 2, tp % 2
    na = ROWS_A
    rows_a, rows_b = pl.ds(0, na), pl.ds(na, 512 - na)
    up = (ctx, 2 * ((y + 1) % 4) + z_lo)
    down = (ctx, 2 * ((y + 3) % 4) + z_lo)
    across = (ctx, tp + 1 - 2 * z_lo)
    blocks = [(2, 0), (1, 0), (3, 0), (0, 0), (2, 1), (1, 1), (3, 1), (0, 1)]

    loads = []
    for i, (r, w) in enumerate(blocks):
        other = z_lo if w else 1 - z_lo
        start = pl.multiple_of((2 * ((y + r) % 4) + other) * 1024, 1024)
        copy = pltpu.make_async_copy(weight_hbm.at[:, pl.ds(start, 1024)], weight.at[i], load_sem.at[i])
        copy.start()
        loads.append(copy)
    barrier = pltpu.get_barrier_semaphore()
    for device in (up, down, across):
        pl.semaphore_signal(barrier, inc=1, device_id=device, device_id_type=MESH)

    def remote(src, dst, send_sem, recv_sem, device):
        copy = pltpu.make_async_remote_copy(
            src, dst, send_sem, recv_sem, device_id=device, device_id_type=MESH
        )
        copy.start()
        return copy

    started = []
    arrive = {}

    def ring(tag, rows, w, m, direction):
        r = 2 if m == 0 else (1 if direction == 0 else 3)
        half = (direction if m in (0, 2) else 1 - direction)
        src = part.at[r, w, pl.ds(2 * half, 2), rows, :]
        slot = 2 * m + direction
        device = up if direction == 0 else down
        if tag == "a":
            copy = remote(src, in_a.at[slot], ya_send.at[slot], ya_recv.at[slot], device)
        else:
            copy = remote(src, in_b.at[w, slot], yb_send.at[w, slot], yb_recv.at[w, slot], device)
        started.append(copy)
        arrive[tag, w, m, direction] = copy

    def across_a(r):
        copy = remote(part.at[r, 0, :, rows_a, :], in_za.at[r], za_send.at[r], za_recv.at[r], across)
        started.append(copy)
        arrive["z", r] = copy

    for i, (r, w) in enumerate(blocks):
        loads[i].wait()

        def tile(j, carry, i=i, r=r, w=w):
            columns = pl.ds(pl.multiple_of(j * 256, 256), 256)
            part[r, w, j] = jnp.dot(mixed_ref[...], weight[i, :, columns], preferred_element_type=F32)
            return carry

        lax.fori_loop(0, 4, tile, 0)
        if i == 0:
            pl.semaphore_wait(barrier, 3)
        if r == 2:
            ring("b", rows_b, w, 0, 0)
            ring("b", rows_b, w, 0, 1)
        elif r == 1:
            ring("b", rows_b, w, 1, 0)
        elif r == 3:
            ring("b", rows_b, w, 1, 1)
        if w == 0:
            across_a(r)

    def add(target, rows, source):
        target[:, rows, :] = target[:, rows, :] + source[...]

    def pass_on(tag, rows, w, inbox):
        for direction, r in ((0, 1), (1, 3)):
            arrive[tag, w, 0, direction].wait_recv()
            add(part.at[r, w, pl.ds(2 * direction, 2)], rows, inbox.at[direction])
            ring(tag, rows, w, 2, direction)

    pass_on("b", rows_b, 0, in_b.at[0])
    pass_on("b", rows_b, 1, in_b.at[1])

    def join_a(r):
        arrive["z", r].wait_recv()
        add(part.at[r, 1], rows_a, in_za.at[r])

    join_a(2)
    ring("a", rows_a, 1, 0, 0)
    ring("a", rows_a, 1, 0, 1)
    join_a(1)
    ring("a", rows_a, 1, 1, 0)
    join_a(3)
    ring("a", rows_a, 1, 1, 1)

    def gather(tag, w, rows, inbox):
        for m in (1, 2):
            for direction in (0, 1):
                arrive[tag, w, m, direction].wait_recv()
                half = direction if m == 2 else 1 - direction
                add(part.at[0, w, pl.ds(2 * half, 2)], rows, inbox.at[2 * m + direction])

    gather("b", 0, rows_b, in_b.at[0])
    last = remote(part.at[0, 0, :, rows_b, :], in_zb, zb_send, zb_recv, across)
    started.append(last)
    join_a(0)
    pass_on("a", rows_a, 1, in_a)
    gather("b", 1, rows_b, in_b.at[1])
    last.wait_recv()
    for j in range(4):
        out_ref[rows_b, 256 * j : 256 * j + 256] = (part[0, 1, j, rows_b, :] + in_zb[j]).astype(BF16)
    gather("a", 1, rows_a, in_a)
    for j in range(4):
        out_ref[rows_a, 256 * j : 256 * j + 256] = part[0, 1, j, rows_a, :].astype(BF16)
    for copy in started:
        copy.wait_send()


def project(mixed, weight):
    vmem = pl.BlockSpec(memory_space=pltpu.VMEM)
    dma = pltpu.SemaphoreType.DMA
    na, nb = ROWS_A, 512 - ROWS_A
    return pl.pallas_call(
        project_kernel,
        name="project",
        out_shape=jax.ShapeDtypeStruct((512, 1024), BF16),
        in_specs=[vmem, pl.BlockSpec(memory_space=pl.ANY)],
        out_specs=vmem,
        scratch_shapes=[
            pltpu.VMEM((8, 1024, 1024), BF16),
            pltpu.VMEM((4, 2, 4, 512, 256), F32),
            pltpu.VMEM((2, 6, 2, nb, 256), F32),
            pltpu.VMEM((6, 2, na, 256), F32),
            pltpu.VMEM((4, 4, na, 256), F32),
            pltpu.VMEM((4, nb, 256), F32),
            dma((8,)), dma((2, 6)), dma((2, 6)), dma((6,)), dma((6,)),
            dma((4,)), dma((4,)), dma, dma,
        ],
        compiler_params=pltpu.CompilerParams(
            collective_id=1, has_side_effects=True, vmem_limit_bytes=60 << 20
        ),
    )(mixed, weight)


def shards(outer_gate, inner_gate, signal, filter_taps, skip_gain, out_weight):
    mixed = convolve(outer_gate, inner_gate, signal, filter_taps, skip_gain)
    return project(mixed, out_weight)


def solution(mesh):
    in_specs = (
        P("ctx", "tp"),
        P("ctx", "tp"),
        P("ctx", "tp"),
        P("ctx", "tp"),
        P("tp"),
        P("tp", None),
    )
    return jax.shard_map(shards, mesh=mesh, in_specs=in_specs, out_specs=P("ctx", "tp"), check_vma=False)
```

```python
import functools
import math

import jax
import jax.numpy as jnp
import numpy as np
from jax import lax
from jax.experimental import pallas as pl
from jax.experimental.pallas import tpu as pltpu
from jax.sharding import PartitionSpec as P

MESH = pl.DeviceIdType.MESH
F32 = jnp.float32
BF16 = jnp.bfloat16

ORDER = ((2, 1), (2, -1), (1, 1), (-1, -1), (1, -1), (-1, 1), (0, 1), (0, -1))
SETS = {"b1": (0, 128), "b2": (128, 192), "a": (320, 192)}


def split(value):
    high = value.astype(BF16)
    low = (value - high.astype(F32)).astype(BF16)
    return high, low


def split_np(value):
    value = np.asarray(value, np.float64)
    high = value.astype(BF16)
    low = (value - high.astype(np.float64)).astype(BF16)
    return np.stack([high, low])


def tables():
    n1 = np.arange(64)[None, :]
    k1 = np.arange(32)[:, None]
    cos = np.cos(2 * np.pi * (n1 * k1 % 64) / 64)
    sin = np.sin(2 * np.pi * (n1 * k1 % 64) / 64)
    ahead = np.stack([cos, -sin], axis=1)
    ahead[0, 1] = (-1.0) ** np.arange(64)
    ahead = ahead.reshape(64, 64)
    back = np.stack([2 * cos, -2 * sin], axis=1)
    back[0, 0] = 1.0
    back[0, 1] = (-1.0) ** np.arange(64)
    back = back.reshape(64, 64).T / 8192
    back = back.reshape(16, 4, 64).transpose(1, 0, 2).reshape(64, 64)
    eye = np.eye(8)
    n2 = np.arange(128)
    angle = 2 * np.pi * (n2[:, None] * n2[None, :] % 128) / 128
    c, s = np.cos(angle), np.sin(angle)
    fwd = np.block([[c, s], [-s, c]])
    inv = np.block([[c, -s], [s, c]])
    turn = 2 * np.pi * (n2[:, None] * np.arange(33)[None, :]) / 8192
    twist = np.zeros((128, 128))
    twist[:, :33] = np.cos(turn)
    twist[:, 64:97] = np.sin(turn)
    return (
        split_np(np.kron(ahead, eye)),
        split_np(np.kron(back, eye)),
        split_np(fwd),
        split_np(inv),
        twist.astype(np.float32),
    )


def dot3(matrix_ref, value):
    high, low = split(value)
    big, small = matrix_ref[0], matrix_ref[1]
    total = jnp.dot(big, low, preferred_element_type=F32)
    total += jnp.dot(small, high, preferred_element_type=F32)
    return total + jnp.dot(big, high, preferred_element_type=F32)


def here():
    ctx, tp = lax.axis_index("ctx"), lax.axis_index("tp")
    return ctx, tp


SEND, RECV, SPEC, PROD, TAPS = 0, 16, 32, 49, 32
BLOCKS = ((2, 0), (1, 0), (3, 0), (0, 0), (2, 1), (1, 1), (3, 1), (0, 1))


def layer_kernel(
    skip_ref, inner_hbm, signal_hbm, taps_hbm, outer_hbm, weight_hbm,
    ahead_hbm, back_hbm, fwd_hbm, inv_hbm, twist_hbm,
    out_ref,
    work, weight, result, home, mixed_ref,
    outer_ref, ahead_ref, back_ref, fwd_ref, inv_ref, twist_ref,
    in_b1, in_b2, in_a, in_za, in_zb1, in_zb2,
    in_sem, load_sem, weight_sem, out_send, out_recv, back_send, back_recv,
    y_send, y_recv, z_send, z_recv,
):
    ctx, tp = here()
    z_hi, x, core = ctx // 8, (ctx // 2) % 4, ctx % 2
    y, z_lo = tp // 2, tp % 2
    z = 2 * z_hi + z_lo
    partner_tp = tp + 1 - 2 * z_lo
    sign = 1 - 2 * core
    up = (ctx, 2 * ((y + 1) % 4) + z_lo)
    down = (ctx, 2 * ((y + 3) % 4) + z_lo)
    across = (ctx, partner_tp)

    quads = []
    for dx, dz in ORDER:
        to_z = (z + dz * sign + 4) % 4
        quads.append((to_z // 2) * 4 + (x + dx * sign + 4) % 4)

    arrays = []
    for step, q in enumerate(quads):
        columns = pl.ds(pl.multiple_of(q * 128, 128), 128)
        copies = [
            pltpu.make_async_copy(
                inner_hbm.at[:, columns], weight.at[7, pl.ds(0, 512), pl.ds(128 * step, 128)], in_sem.at[step, 0]
            ),
            pltpu.make_async_copy(
                signal_hbm.at[:, columns], weight.at[7, pl.ds(512, 512), pl.ds(128 * step, 128)], in_sem.at[step, 1]
            ),
            pltpu.make_async_copy(taps_hbm.at[:, columns], work.at[TAPS + step], in_sem.at[step, 2]),
        ]
        for copy in copies:
            copy.start()
        arrays.append(copies)

    barrier = pltpu.get_barrier_semaphore()
    for q in quads:
        for k in (0, 1):
            pl.semaphore_signal(barrier, inc=1, device_id=(2 * q + k, partner_tp), device_id_type=MESH)
    for device in (up, down):
        pl.semaphore_signal(barrier, inc=1, device_id=device, device_id_type=MESH)

    loads = []
    for i, (src, dst) in enumerate(
        (
            (ahead_hbm, ahead_ref), (fwd_hbm, fwd_ref), (inv_hbm, inv_ref),
            (back_hbm, back_ref), (twist_hbm, twist_ref), (outer_hbm, outer_ref),
        )
    ):
        copy = pltpu.make_async_copy(src, dst, load_sem.at[i])
        copy.start()
        loads.append(copy)

    def load_weight(i):
        r, w = BLOCKS[i]
        other = z_lo if w else 1 - z_lo
        start = pl.multiple_of((2 * ((y + r) % 4) + other) * 1024, 1024)
        copy = pltpu.make_async_copy(weight_hbm.at[:, pl.ds(start, 1024)], weight.at[i], weight_sem.at[i])
        copy.start()
        return copy

    weights = [load_weight(i) for i in range(7)]

    lane = lax.broadcasted_iota(jnp.int32, (128, 128), 1)
    first = lane < 64
    row0 = lax.broadcasted_iota(jnp.int32, (128, 128), 0)
    sends = []
    for step, q in enumerate(quads):
        skip = skip_ref[:, pl.ds(pl.multiple_of(q * 128, 128), 128)]
        for copy in arrays[step]:
            copy.wait()

        def pack(i, carry, step=step, skip=skip, q=q):
            start = pl.multiple_of(i * 128, 128)
            rows = pl.ds(start, 128)
            columns = pl.ds(128 * step, 128)
            gated = weight[7, rows, columns].astype(F32) * weight[7, pl.ds(512 + start, 128), columns].astype(F32)
            taps = work[TAPS + step, rows, :] + jnp.where(row0 + i * 128 + ctx * 512 == 0, skip, 0.0)
            work[SEND + 2 * q, rows, :] = jnp.where(first, gated, pltpu.roll(taps, 64, 1))
            work[SEND + 2 * q + 1, rows, :] = jnp.where(first, pltpu.roll(gated, 64, 1), taps)
            return carry

        lax.fori_loop(0, 4, pack, 0)
        if step == 0:
            pl.semaphore_wait(barrier, 18)
        for dk in (0, 1):
            k = (core + dk) % 2
            copy = pltpu.make_async_remote_copy(
                work.at[SEND + 2 * q + k], work.at[RECV + ctx],
                out_send.at[2 * step + dk], out_recv.at[2 * step + dk],
                device_id=(2 * q + k, partner_tp), device_id_type=MESH,
            )
            copy.start()
            sends.append(copy)
    weights.append(load_weight(7))
    for copy in loads:
        copy.wait()
    for copy in sends:
        copy.wait_recv()

    first8 = lax.broadcasted_iota(jnp.int32, (8, 128), 1) < 64

    def put_spec(k1, part, half, a, value):
        start = (k1 % 2) * 256 + part * 128 + half * 64 + a * 8
        work[SPEC + k1 // 2, pl.ds(pl.multiple_of(start, 8), 8), :] = value

    def prod_at(pair, part, rows):
        start = (pair % 2) * 256 + part * 128 + rows
        return work[PROD + pair // 2, pl.ds(pl.multiple_of(start, 8), 8), :]

    def stage_one(a, carry):
        parts = []
        for half in (0, 1):
            start = pl.multiple_of(half * 64 + a * 8, 8)
            parts.append(
                jnp.concatenate(
                    [
                        work[RECV + s, pl.ds(pl.multiple_of(j * 128 + start, 8), 8), :]
                        for s in range(16)
                        for j in range(4)
                    ],
                    axis=0,
                )
            )
        out = dot3(ahead_ref, jnp.concatenate(parts, axis=1))
        for half in (0, 1):
            rows = pl.ds(pl.multiple_of(half * 64 + a * 8, 8), 8)
            twist = twist_ref[rows, :]
            for k1 in range(33):
                if k1 == 0:
                    put_spec(0, 0, half, a, out[0:8, half * 128 : half * 128 + 128])
                    put_spec(0, 1, half, a, jnp.zeros((8, 128), F32))
                    continue
                cos, sin = twist[:, k1 : k1 + 1], twist[:, 64 + k1 : 65 + k1]
                if k1 == 32:
                    real = out[8:16, half * 128 : half * 128 + 128]
                    put_spec(32, 0, half, a, real * cos)
                    put_spec(32, 1, half, a, -(real * sin))
                    continue
                real = out[16 * k1 : 16 * k1 + 8, half * 128 : half * 128 + 128]
                imag = out[16 * k1 + 8 : 16 * k1 + 16, half * 128 : half * 128 + 128]
                put_spec(k1, 0, half, a, real * cos + imag * sin)
                put_spec(k1, 1, half, a, imag * cos - real * sin)
        return carry

    lax.fori_loop(0, 8, stage_one, 0)

    def product(out, j):
        real, imag = out[:128, 128 * j : 128 * j + 128], out[128:, 128 * j : 128 * j + 128]
        real2, imag2 = pltpu.roll(real, 64, 1), pltpu.roll(imag, 64, 1)
        return jnp.concatenate([real * real2 - imag * imag2, real * imag2 + imag * real2], axis=0)

    first256 = lax.broadcasted_iota(jnp.int32, (256, 128), 1) < 64

    def stage_two(i, carry):
        value = jnp.concatenate([work[SPEC + 2 * i + j // 2, 256 * (j % 2) : 256 * (j % 2) + 256, :] for j in range(4)], axis=1)
        out = dot3(fwd_ref, value)
        pairs = [
            jnp.where(first256, product(out, 2 * j), product(out, 2 * j + 1)) for j in range(2)
        ]
        out = dot3(inv_ref, jnp.concatenate(pairs, axis=1))
        for j in range(2):
            work[PROD + i, 256 * j : 256 * j + 256, :] = out[:, 128 * j : 128 * j + 128]
        return carry

    lax.fori_loop(0, 8, stage_two, 0)
    out = dot3(fwd_ref, work[SPEC + 16, 0:256, :])
    work[PROD + 8, 0:256, :] = dot3(inv_ref, product(out, 0))

    def stage_three(a2, carry):
        sides = []
        for side in (0, 1):
            a = 2 * a2 + side
            low = pl.ds(pl.multiple_of(a * 8, 8), 8)
            high = pl.ds(pl.multiple_of(64 + a * 8, 8), 8)
            near, far = twist_ref[low, :], twist_ref[high, :]

            def turn(k1):
                cos = jnp.where(first8, near[:, k1 : k1 + 1], far[:, k1 : k1 + 1])
                sin = jnp.where(first8, near[:, 64 + k1 : 65 + k1], far[:, 64 + k1 : 65 + k1])
                return cos, sin

            pieces = []
            for pair in range(16):
                here_re, here_im = prod_at(pair, 0, a * 8), prod_at(pair, 1, a * 8)
                next_re, next_im = prod_at(pair, 0, 64 + a * 8), prod_at(pair, 1, 64 + a * 8)
                for odd in (0, 1):
                    k1 = 2 * pair + odd
                    if odd:
                        real = jnp.where(first8, pltpu.roll(here_re, 64, 1), next_re)
                        imag = jnp.where(first8, pltpu.roll(here_im, 64, 1), next_im)
                    else:
                        real = jnp.where(first8, here_re, pltpu.roll(next_re, 64, 1))
                        imag = jnp.where(first8, here_im, pltpu.roll(next_im, 64, 1))
                    if k1 == 0:
                        pieces.append(real)
                        real = jnp.where(first8, prod_at(16, 0, a * 8), prod_at(16, 0, 64 + a * 8))
                        imag = jnp.where(first8, prod_at(16, 1, a * 8), prod_at(16, 1, 64 + a * 8))
                        cos, sin = turn(32)
                        pieces.append(real * cos - imag * sin)
                        continue
                    cos, sin = turn(k1)
                    pieces.append(real * cos - imag * sin)
                    pieces.append(real * sin + imag * cos)
            sides.append(jnp.concatenate(pieces, axis=0))
        out = dot3(back_ref, jnp.concatenate(sides, axis=1))
        for side in (0, 1):
            rows = pl.ds(pl.multiple_of((2 * a2 + side) * 8, 8), 8)
            result[:, :, rows, :] = out[:, 128 * side : 128 * side + 128].reshape(4, 16, 8, 128)
        return carry

    lax.fori_loop(0, 4, stage_three, 0)

    for copy in sends:
        copy.wait_send()
    returns = [[], []]
    for part, (begin, count) in enumerate(((0, 1), (1, 3))):
        for step, q in enumerate(quads):
            for dk in (0, 1):
                other = 2 * q + (core + dk) % 2
                copy = pltpu.make_async_remote_copy(
                    result.at[pl.ds(begin, count), other], home.at[ctx, pl.ds(begin, count)],
                    back_send.at[part, 2 * step + dk], back_recv.at[part, 2 * step + dk],
                    device_id=(other, partner_tp), device_id_type=MESH,
                )
                copy.start()
                returns[part].append(copy)

    first64 = lax.broadcasted_iota(jnp.int32, (64, 128), 1) < 64

    def gate(j, carry):
        base = pl.multiple_of(j * 128, 128)
        for q in range(8):
            even, odd = home[2 * q, j], home[2 * q + 1, j]
            for rows, conv in (
                (pl.ds(base, 64), jnp.where(first64, even, pltpu.roll(odd, 64, 1))),
                (pl.ds(base + 64, 64), jnp.where(first64, pltpu.roll(even, 64, 1), odd)),
            ):
                gated = outer_ref[rows, 128 * q : 128 * q + 128].astype(F32) * conv
                mixed_ref[rows, 128 * q : 128 * q + 128] = gated.astype(BF16)
        return carry

    started = []
    arrive = {}
    inboxes = {"b1": in_b1, "b2": in_b2, "a": in_a}
    lane_of = {("b1", 0): 0, ("b1", 1): 1, ("b2", 0): 2, ("b2", 1): 3, ("a", 1): 4}

    def rows_of(name):
        return pl.ds(*SETS[name])

    def slots(r, w, half=None):
        block = 8 * BLOCKS.index((r, w))
        return pl.ds(block, 8) if half is None else pl.ds(block + 4 * half, 4)

    def inbox(name, w, slot):
        return in_a.at[slot] if name == "a" else inboxes[name].at[w, slot]

    def remote(src, dst, send_sem, recv_sem, device):
        copy = pltpu.make_async_remote_copy(
            src, dst, send_sem, recv_sem, device_id=device, device_id_type=MESH
        )
        copy.start()
        started.append(copy)
        return copy

    def ring(name, w, m, direction):
        r = 2 if m == 0 else (1 if direction == 0 else 3)
        half = direction if m in (0, 2) else 1 - direction
        slot = 2 * m + direction
        at = lane_of[name, w]
        arrive[name, w, m, direction] = remote(
            work.at[slots(r, w, half), rows_of(name), :], inbox(name, w, slot),
            y_send.at[at, slot], y_recv.at[at, slot], up if direction == 0 else down,
        )

    def own(name, i):
        r, w = BLOCKS[i]
        if r == 2:
            ring(name, w, 0, 0)
            ring(name, w, 0, 1)
        elif r == 1:
            ring(name, w, 1, 0)
        elif r == 3:
            ring(name, w, 1, 1)

    def across_a(r):
        arrive["z", r] = remote(
            work.at[slots(r, 0), rows_of("a"), :], in_za.at[r], z_send.at[r], z_recv.at[r], across
        )

    def multiply(i, begin, count):
        def tile(j, carry):
            columns = pl.ds(pl.multiple_of(j * 256, 256), 256)
            rows = pl.ds(begin, count)
            value = jnp.dot(mixed_ref[rows, :], weight[i, :, columns], preferred_element_type=F32)
            work[8 * i + 2 * j, rows, :] = value[:, :128]
            work[8 * i + 2 * j + 1, rows, :] = value[:, 128:]
            return carry

        lax.fori_loop(0, 4, tile, 0)

    def add(target, name, source):
        rows = rows_of(name)
        work[target, rows, :] = work[target, rows, :] + source[...]

    def pass_on(name, w):
        for direction, r in ((0, 1), (1, 3)):
            arrive[name, w, 0, direction].wait_recv()
            add(slots(r, w, direction), name, inbox(name, w, direction))
            ring(name, w, 2, direction)

    def join_a(r):
        arrive["z", r].wait_recv()
        add(slots(r, 1), "a", in_za.at[r])

    def gather(name, w):
        for m in (1, 2):
            for direction in (0, 1):
                arrive[name, w, m, direction].wait_recv()
                half = direction if m == 2 else 1 - direction
                add(slots(0, w, half), name, inbox(name, w, 2 * m + direction))

    def across_b(name, box, at):
        return remote(work.at[slots(0, 0), rows_of(name), :], box, z_send.at[at], z_recv.at[at], across)

    def finish(name, box=None):
        rows = rows_of(name)
        for j in range(8):
            value = work[8 * BLOCKS.index((0, 1)) + j, rows, :]
            if box is not None:
                value = value + box[j]
            out_ref[rows, 128 * j : 128 * j + 128] = value.astype(BF16)

    for copy in returns[0]:
        copy.wait_recv()
    lax.fori_loop(0, 1, gate, 0)
    for i in range(8):
        weights[i].wait()
        multiply(i, 0, 128)
        own("b1", i)
    for copy in returns[1]:
        copy.wait_recv()
    lax.fori_loop(1, 4, gate, 0)
    for i in range(8):
        multiply(i, 128, 384)
        if BLOCKS[i][1] == 0:
            across_a(BLOCKS[i][0])
        own("b2", i)
        if i == 1:
            pass_on("b1", 0)
    pass_on("b1", 1)
    pass_on("b2", 0)
    join_a(2)
    ring("a", 1, 0, 0)
    ring("a", 1, 0, 1)
    gather("b1", 0)
    last1 = across_b("b1", in_zb1, 4)
    pass_on("b2", 1)
    join_a(1)
    ring("a", 1, 1, 0)
    join_a(3)
    ring("a", 1, 1, 1)
    gather("b1", 1)
    gather("b2", 0)
    last2 = across_b("b2", in_zb2, 5)
    last1.wait_recv()
    finish("b1", in_zb1)
    join_a(0)
    pass_on("a", 1)
    gather("b2", 1)
    last2.wait_recv()
    finish("b2", in_zb2)
    gather("a", 1)
    finish("a")
    for copy in returns[0] + returns[1] + started:
        copy.wait_send()


def shards(outer_gate, inner_gate, signal, filter_taps, skip_gain, out_weight):
    vmem = pl.BlockSpec(memory_space=pltpu.VMEM)
    hbm = pl.BlockSpec(memory_space=pl.ANY)
    dma = pltpu.SemaphoreType.DMA
    n1, n2, na = SETS["b1"][1], SETS["b2"][1], SETS["a"][1]
    return pl.pallas_call(
        layer_kernel,
        name="layer",
        out_shape=jax.ShapeDtypeStruct((512, 1024), BF16),
        in_specs=[vmem] + [hbm] * 10,
        out_specs=vmem,
        scratch_shapes=[
            pltpu.VMEM((64, 512, 128), F32),
            pltpu.VMEM((8, 1024, 1024), BF16),
            pltpu.VMEM((4, 16, 64, 128), F32),
            pltpu.VMEM((16, 4, 64, 128), F32),
            pltpu.VMEM((512, 1024), BF16),
            pltpu.VMEM((512, 1024), BF16),
            pltpu.VMEM((2, 512, 512), BF16),
            pltpu.VMEM((2, 512, 512), BF16),
            pltpu.VMEM((2, 256, 256), BF16),
            pltpu.VMEM((2, 256, 256), BF16),
            pltpu.VMEM((128, 128), F32),
            pltpu.VMEM((2, 6, 4, n1, 128), F32),
            pltpu.VMEM((2, 6, 4, n2, 128), F32),
            pltpu.VMEM((6, 4, na, 128), F32),
            pltpu.VMEM((4, 8, na, 128), F32),
            pltpu.VMEM((8, n1, 128), F32),
            pltpu.VMEM((8, n2, 128), F32),
            dma((8, 3)), dma((6,)), dma((8,)), dma((16,)), dma((16,)), dma((2, 16)), dma((2, 16)),
            dma((5, 6)), dma((5, 6)), dma((6,)), dma((6,)),
        ],
        compiler_params=pltpu.CompilerParams(
            collective_id=0, has_side_effects=True, vmem_limit_bytes=62 << 20
        ),
    )(
        skip_gain.reshape(1, -1), inner_gate, signal, filter_taps, outer_gate, out_weight, *tables(),
    )


def solution(mesh):
    in_specs = (
        P("ctx", "tp"),
        P("ctx", "tp"),
        P("ctx", "tp"),
        P("ctx", "tp"),
        P("tp"),
        P("tp", None),
    )
    return jax.shard_map(shards, mesh=mesh, in_specs=in_specs, out_specs=P("ctx", "tp"), check_vma=False)
```

```python
import functools
import math

import jax
import jax.numpy as jnp
import numpy as np
from jax import lax
from jax.experimental import pallas as pl
from jax.experimental.pallas import tpu as pltpu
from jax.sharding import PartitionSpec as P

MESH = pl.DeviceIdType.MESH
F32 = jnp.float32
BF16 = jnp.bfloat16

ORDER = ((2, 1), (2, -1), (1, 1), (-1, -1), (1, -1), (-1, 1), (0, 1), (0, -1))
SETS = {"b": (0, 128), "a1": (128, 128), "a2": (256, 128), "a3": (384, 128)}
AS = ("a1", "a2", "a3")
UNITS = ((2, 0), (2, 1), (1, 1), (3, 0), (1, 0), (3, 1), (0, 0), (0, 1))
SLOT = {2: 0, 1: 1, 3: 2, 0: 3}
BY_Z = (True, True, False, False, False, False, True, True)


def split(value):
    high = value.astype(BF16)
    low = (value - high.astype(F32)).astype(BF16)
    return high, low


def split_np(value):
    value = np.asarray(value, np.float64)
    high = value.astype(BF16)
    low = (value - high.astype(np.float64)).astype(BF16)
    return np.stack([high, low])


def tables():
    n1 = np.arange(64)[None, :]
    k1 = np.arange(32)[:, None]
    cos = np.cos(2 * np.pi * (n1 * k1 % 64) / 64)
    sin = np.sin(2 * np.pi * (n1 * k1 % 64) / 64)
    ahead = np.stack([cos, -sin], axis=1)
    ahead[0, 1] = (-1.0) ** np.arange(64)
    ahead = ahead.reshape(64, 64)
    back = np.stack([2 * cos, -2 * sin], axis=1)
    back[0, 0] = 1.0
    back[0, 1] = (-1.0) ** np.arange(64)
    back = back.reshape(64, 64).T / 8192
    back = back.reshape(16, 4, 64).transpose(1, 0, 2).reshape(64, 64)
    eye = np.eye(8)
    n2 = np.arange(128)
    angle = 2 * np.pi * (n2[:, None] * n2[None, :] % 128) / 128
    c, s = np.cos(angle), np.sin(angle)
    fwd = np.block([[c, s], [-s, c]])
    inv = np.block([[c, -s], [s, c]])
    turn = 2 * np.pi * (n2[:, None] * np.arange(33)[None, :]) / 8192
    twist = np.zeros((128, 128))
    twist[:, :33] = np.cos(turn)
    twist[:, 64:97] = np.sin(turn)
    return (
        split_np(np.kron(ahead, eye)),
        split_np(np.kron(back, eye)),
        split_np(fwd),
        split_np(inv),
        twist.astype(np.float32),
    )


def dot3(matrix_ref, value):
    high, low = split(value)
    big, small = matrix_ref[0], matrix_ref[1]
    total = jnp.dot(big, low, preferred_element_type=F32)
    total += jnp.dot(small, high, preferred_element_type=F32)
    return total + jnp.dot(big, high, preferred_element_type=F32)


def here():
    ctx, tp = lax.axis_index("ctx"), lax.axis_index("tp")
    return ctx, tp


SEND, RECV, SPEC, PROD, TAPS = 0, 16, 32, 49, 32
BLOCKS = ((2, 0), (1, 0), (3, 0), (0, 0), (2, 1), (1, 1), (3, 1), (0, 1))


def layer_kernel(
    skip_ref, inner_hbm, signal_hbm, taps_hbm, outer_hbm, weight_hbm,
    ahead_hbm, back_hbm, fwd_hbm, inv_hbm, twist_hbm,
    out_hbm, wide,
    work, weight, result, home, mixed_ref, out_ref,
    outer_ref, ahead_ref, back_ref, fwd_ref, inv_ref, twist_ref,
    in_b, in_a, in_zb, give, take, other_mixed, share,
    in_sem, load_sem, weight_sem, wide_sem, out_sem, out_send, out_recv, back_send, back_recv,
    y_send, y_recv, z_send, z_recv, wz_send, wz_recv, wx_send, wx_recv, wc_send, wc_recv,
):
    ctx, tp = here()
    z_hi, x, core = ctx // 8, (ctx // 2) % 4, ctx % 2
    y, z_lo = tp // 2, tp % 2
    z = 2 * z_hi + z_lo
    partner_tp = tp + 1 - 2 * z_lo
    sign = 1 - 2 * core
    up = (ctx, 2 * ((y + 1) % 4) + z_lo)
    down = (ctx, 2 * ((y + 3) % 4) + z_lo)
    across = (ctx, partner_tp)
    sides = [(8 * ((z + d) % 4 // 2) + 2 * x + core, partner_tp) for d in (1, 3)]
    rights = [(8 * z_hi + 2 * ((x + d) % 4) + core, tp) for d in (1, 3, 2)]
    twin = (ctx + sign, tp)

    quads = []
    for dx, dz in ORDER:
        to_z = (z + dz * sign + 4) % 4
        quads.append((to_z // 2) * 4 + (x + dx * sign + 4) % 4)

    arrays = []
    for step, q in enumerate(quads):
        columns = pl.ds(pl.multiple_of(q * 128, 128), 128)
        copies = [
            pltpu.make_async_copy(
                inner_hbm.at[:, columns], weight.at[7, pl.ds(0, 512), pl.ds(128 * step, 128)], in_sem.at[step, 0]
            ),
            pltpu.make_async_copy(
                signal_hbm.at[:, columns], weight.at[7, pl.ds(512, 512), pl.ds(128 * step, 128)], in_sem.at[step, 1]
            ),
            pltpu.make_async_copy(taps_hbm.at[:, columns], work.at[TAPS + step], in_sem.at[step, 2]),
        ]
        for copy in copies:
            copy.start()
        arrays.append(copies)

    barrier = pltpu.get_barrier_semaphore()
    for q in quads:
        for k in (0, 1):
            pl.semaphore_signal(barrier, inc=1, device_id=(2 * q + k, partner_tp), device_id_type=MESH)
    for device in [up, down, twin] + rights:
        pl.semaphore_signal(barrier, inc=1, device_id=device, device_id_type=MESH)

    loads = []
    for i, (src, dst) in enumerate(
        (
            (ahead_hbm, ahead_ref), (fwd_hbm, fwd_ref), (inv_hbm, inv_ref),
            (back_hbm, back_ref), (twist_hbm, twist_ref), (outer_hbm, outer_ref),
        )
    ):
        copy = pltpu.make_async_copy(src, dst, load_sem.at[i])
        copy.start()
        loads.append(copy)

    def load_weight(i):
        r, w = BLOCKS[i]
        other = z_lo if w else 1 - z_lo
        start = pl.multiple_of((2 * ((y + r) % 4) + other) * 1024, 1024)
        copy = pltpu.make_async_copy(weight_hbm.at[:, pl.ds(start, 1024)], weight.at[i], weight_sem.at[i])
        copy.start()
        return copy

    weights = [load_weight(i) for i in range(7)]

    lane = lax.broadcasted_iota(jnp.int32, (128, 128), 1)
    first = lane < 64
    row0 = lax.broadcasted_iota(jnp.int32, (128, 128), 0)
    sends = []
    for step, q in enumerate(quads):
        skip = skip_ref[:, pl.ds(pl.multiple_of(q * 128, 128), 128)]
        for copy in arrays[step]:
            copy.wait()

        def pack(i, carry, step=step, skip=skip, q=q):
            start = pl.multiple_of(i * 128, 128)
            rows = pl.ds(start, 128)
            columns = pl.ds(128 * step, 128)
            gated = weight[7, rows, columns].astype(F32) * weight[7, pl.ds(512 + start, 128), columns].astype(F32)
            taps = work[TAPS + step, rows, :] + jnp.where(row0 + i * 128 + ctx * 512 == 0, skip, 0.0)
            work[SEND + 2 * q, rows, :] = jnp.where(first, gated, pltpu.roll(taps, 64, 1))
            work[SEND + 2 * q + 1, rows, :] = jnp.where(first, pltpu.roll(gated, 64, 1), taps)
            return carry

        lax.fori_loop(0, 4, pack, 0)
        if step == 0:
            pl.semaphore_wait(barrier, 22)
        for dk in (0, 1):
            k = (core + dk) % 2
            copy = pltpu.make_async_remote_copy(
                work.at[SEND + 2 * q + k], work.at[RECV + ctx],
                out_send.at[2 * step + dk], out_recv.at[2 * step + dk],
                device_id=(2 * q + k, partner_tp), device_id_type=MESH,
            )
            copy.start()
            sends.append(copy)
    weights.append(load_weight(7))
    for copy in loads:
        copy.wait()
    mine = [pl.multiple_of(256 * ((x + d) % 4) + 128 * core + 64 * z_hi, 64) for d in (0, 2)]
    for i in range(4):
        weights[i].wait()
    for u, (r, half) in enumerate(UNITS):
        for c in range(4):
            columns = slice(512 * half + 128 * c, 512 * half + 128 * c + 128)
            for p in (0, 1):
                share[u, p, c] = weight[SLOT[r], pl.ds(mine[p], 64), columns].astype(F32)
    for copy in sends:
        copy.wait_recv()

    started = []

    def remote(src, dst, send_sem, recv_sem, device):
        copy = pltpu.make_async_remote_copy(
            src, dst, send_sem, recv_sem, device_id=device, device_id_type=MESH
        )
        copy.start()
        started.append(copy)
        return copy

    wz, wx, wc = {}, {}, {}

    def give_z(u):
        for p in range(1 + BY_Z[u]):
            for h in (0, 1):
                wz[u, p, h] = remote(
                    share.at[u, p], wide.at[u, :, pl.ds(mine[p], 64)],
                    wz_send.at[u, 2 * p + h], wz_recv.at[u, 2 * p + h], sides[h],
                )

    def quarter(u, d):
        return wide.at[u, :, pl.ds(pl.multiple_of(256 * ((x + d) % 4) + 128 * core, 128), 128)]

    def give_core(u, d):
        wc[u, d] = remote(quarter(u, d), quarter(u, d), wc_send.at[u, d], wc_recv.at[u, d], twin)

    def spread(u):
        for h in (0, 1):
            wz[u, 0, h].wait_recv()
        for n in range(3 - BY_Z[u]):
            wx[u, n] = remote(quarter(u, 0), quarter(u, 0), wx_send.at[u, n], wx_recv.at[u, n], rights[n])
        give_core(u, 0)
        if BY_Z[u]:
            for h in (0, 1):
                wz[u, 1, h].wait_recv()
            give_core(u, 2)

    def pair_up(u):
        for n, d in enumerate((3, 1) if BY_Z[u] else (3, 1, 2)):
            wx[u, n].wait_recv()
            give_core(u, d)

    def fetch(u):
        for n in range(4):
            wc[u, n].wait_recv()
        copy = pltpu.make_async_copy(wide.at[u], (result, home)[u % 2], wide_sem.at[u])
        copy.start()
        return copy

    def settle(u, copy):
        copy.wait()
        r, half = UNITS[u]
        box = (result, home)[u % 2]

        def convert(i, carry):
            rows = pl.ds(pl.multiple_of(i * 128, 128), 128)
            for c in range(4):
                columns = slice(512 * half + 128 * c, 512 * half + 128 * c + 128)
                weight[SLOT[r], rows, columns] = box[c, rows, :].astype(BF16)
            return carry

        lax.fori_loop(0, 8, convert, 0)

    for u in range(5):
        give_z(u)

    first8 = lax.broadcasted_iota(jnp.int32, (8, 128), 1) < 64

    def put_spec(k1, part, half, a, value):
        start = (k1 % 2) * 256 + part * 128 + half * 64 + a * 8
        work[SPEC + k1 // 2, pl.ds(pl.multiple_of(start, 8), 8), :] = value

    def prod_at(pair, part, rows):
        start = (pair % 2) * 256 + part * 128 + rows
        return work[PROD + pair // 2, pl.ds(pl.multiple_of(start, 8), 8), :]

    def stage_one(a, carry):
        parts = []
        for half in (0, 1):
            start = pl.multiple_of(half * 64 + a * 8, 8)
            parts.append(
                jnp.concatenate(
                    [
                        work[RECV + s, pl.ds(pl.multiple_of(j * 128 + start, 8), 8), :]
                        for s in range(16)
                        for j in range(4)
                    ],
                    axis=0,
                )
            )
        out = dot3(ahead_ref, jnp.concatenate(parts, axis=1))
        for half in (0, 1):
            rows = pl.ds(pl.multiple_of(half * 64 + a * 8, 8), 8)
            twist = twist_ref[rows, :]
            for k1 in range(33):
                if k1 == 0:
                    put_spec(0, 0, half, a, out[0:8, half * 128 : half * 128 + 128])
                    put_spec(0, 1, half, a, jnp.zeros((8, 128), F32))
                    continue
                cos, sin = twist[:, k1 : k1 + 1], twist[:, 64 + k1 : 65 + k1]
                if k1 == 32:
                    real = out[8:16, half * 128 : half * 128 + 128]
                    put_spec(32, 0, half, a, real * cos)
                    put_spec(32, 1, half, a, -(real * sin))
                    continue
                real = out[16 * k1 : 16 * k1 + 8, half * 128 : half * 128 + 128]
                imag = out[16 * k1 + 8 : 16 * k1 + 16, half * 128 : half * 128 + 128]
                put_spec(k1, 0, half, a, real * cos + imag * sin)
                put_spec(k1, 1, half, a, imag * cos - real * sin)
        return carry

    lax.fori_loop(0, 8, stage_one, 0)

    def product(out, j):
        real, imag = out[:128, 128 * j : 128 * j + 128], out[128:, 128 * j : 128 * j + 128]
        real2, imag2 = pltpu.roll(real, 64, 1), pltpu.roll(imag, 64, 1)
        return jnp.concatenate([real * real2 - imag * imag2, real * imag2 + imag * real2], axis=0)

    first256 = lax.broadcasted_iota(jnp.int32, (256, 128), 1) < 64

    def stage_two(i, carry):
        value = jnp.concatenate([work[SPEC + 2 * i + j // 2, 256 * (j % 2) : 256 * (j % 2) + 256, :] for j in range(4)], axis=1)
        out = dot3(fwd_ref, value)
        pairs = [
            jnp.where(first256, product(out, 2 * j), product(out, 2 * j + 1)) for j in range(2)
        ]
        out = dot3(inv_ref, jnp.concatenate(pairs, axis=1))
        for j in range(2):
            work[PROD + i, 256 * j : 256 * j + 256, :] = out[:, 128 * j : 128 * j + 128]
        return carry

    lax.fori_loop(0, 4, stage_two, 0)
    spread(0)
    lax.fori_loop(4, 8, stage_two, 0)
    spread(1)
    out = dot3(fwd_ref, work[SPEC + 16, 0:256, :])
    work[PROD + 8, 0:256, :] = dot3(inv_ref, product(out, 0))

    def stage_three(a2, carry):
        sides = []
        for side in (0, 1):
            a = 2 * a2 + side
            low = pl.ds(pl.multiple_of(a * 8, 8), 8)
            high = pl.ds(pl.multiple_of(64 + a * 8, 8), 8)
            near, far = twist_ref[low, :], twist_ref[high, :]

            def turn(k1):
                cos = jnp.where(first8, near[:, k1 : k1 + 1], far[:, k1 : k1 + 1])
                sin = jnp.where(first8, near[:, 64 + k1 : 65 + k1], far[:, 64 + k1 : 65 + k1])
                return cos, sin

            pieces = []
            for pair in range(16):
                here_re, here_im = prod_at(pair, 0, a * 8), prod_at(pair, 1, a * 8)
                next_re, next_im = prod_at(pair, 0, 64 + a * 8), prod_at(pair, 1, 64 + a * 8)
                for odd in (0, 1):
                    k1 = 2 * pair + odd
                    if odd:
                        real = jnp.where(first8, pltpu.roll(here_re, 64, 1), next_re)
                        imag = jnp.where(first8, pltpu.roll(here_im, 64, 1), next_im)
                    else:
                        real = jnp.where(first8, here_re, pltpu.roll(next_re, 64, 1))
                        imag = jnp.where(first8, here_im, pltpu.roll(next_im, 64, 1))
                    if k1 == 0:
                        pieces.append(real)
                        real = jnp.where(first8, prod_at(16, 0, a * 8), prod_at(16, 0, 64 + a * 8))
                        imag = jnp.where(first8, prod_at(16, 1, a * 8), prod_at(16, 1, 64 + a * 8))
                        cos, sin = turn(32)
                        pieces.append(real * cos - imag * sin)
                        continue
                    cos, sin = turn(k1)
                    pieces.append(real * cos - imag * sin)
                    pieces.append(real * sin + imag * cos)
            sides.append(jnp.concatenate(pieces, axis=0))
        out = dot3(back_ref, jnp.concatenate(sides, axis=1))
        for side in (0, 1):
            value = out[:, 128 * side : 128 * side + 128].reshape(4, 16, 8, 128)
            for s in range(16):
                result[:, pl.ds(pl.multiple_of(64 * s + (2 * a2 + side) * 8, 8), 8), :] = value[:, s]
        return carry

    lax.fori_loop(0, 4, stage_three, 0)

    for copy in sends:
        copy.wait_send()
    returns = [[], [], [], []]

    def give_back(part):
        for step, q in enumerate(quads):
            for dk in (0, 1):
                other = 2 * q + (core + dk) % 2
                copy = pltpu.make_async_remote_copy(
                    result.at[part, pl.ds(pl.multiple_of(64 * other, 64), 64)],
                    home.at[part, pl.ds(pl.multiple_of(64 * ctx, 64), 64)],
                    back_send.at[part, 2 * step + dk], back_recv.at[part, 2 * step + dk],
                    device_id=(other, partner_tp), device_id_type=MESH,
                )
                copy.start()
                returns[part].append(copy)

    def receive(part):
        for copy in returns[part]:
            copy.wait_recv()

    give_back(0)
    give_back(1)
    receive(0)
    give_back(2)
    first64 = lax.broadcasted_iota(jnp.int32, (64, 128), 1) < 64

    def gate(j, carry, keep=True):
        base = pl.multiple_of(j * 128, 128)
        for q in range(8):
            even, odd = home[j, 128 * q : 128 * q + 64, :], home[j, 128 * q + 64 : 128 * q + 128, :]
            for rows, conv in (
                (pl.ds(base, 64), jnp.where(first64, even, pltpu.roll(odd, 64, 1))),
                (pl.ds(base + 64, 64), jnp.where(first64, pltpu.roll(even, 64, 1), odd)),
            ):
                gated = outer_ref[rows, 128 * q : 128 * q + 128].astype(F32) * conv
                rounded = gated.astype(BF16)
                mixed_ref[rows, 128 * q : 128 * q + 128] = rounded
                if keep:
                    begin = 64 * (rows.start != base)
                    give[j - 1, pl.ds(begin, 64), 128 * q : 128 * q + 128] = rounded.astype(F32)
        return carry

    arrive = {}
    lane_of = {("b", 0): 0, ("b", 1): 1, ("a1", 1): 2, ("a2", 1): 3, ("a3", 1): 4}

    def rows_of(name):
        return pl.ds(*SETS[name])

    def slots(r, w, half=None):
        block = 8 * BLOCKS.index((r, w))
        return pl.ds(block, 8) if half is None else pl.ds(block + 4 * half, 4)

    def inbox(name, w, slot):
        return in_b.at[w, slot] if name == "b" else in_a.at[AS.index(name), slot]

    def ring(name, w, m, direction):
        r = 2 if m == 0 else (1 if direction == 0 else 3)
        half = direction if m in (0, 2) else 1 - direction
        slot = 2 * m + direction
        at = lane_of[name, w]
        arrive[name, w, m, direction] = remote(
            work.at[slots(r, w, half), rows_of(name), :], inbox(name, w, slot),
            y_send.at[at, slot], y_recv.at[at, slot], up if direction == 0 else down,
        )

    def own(name, i):
        r, w = BLOCKS[i]
        if r == 2:
            ring(name, w, 0, 0)
            ring(name, w, 0, 1)
        elif r == 1:
            ring(name, w, 1, 0)
        elif r == 3:
            ring(name, w, 1, 1)

    def multiply(i, begin, count):
        def tile(j, carry):
            columns = pl.ds(pl.multiple_of(j * 256, 256), 256)
            rows = pl.ds(begin, count)
            value = jnp.dot(mixed_ref[rows, :], weight[i, :, columns], preferred_element_type=F32)
            work[8 * i + 2 * j, rows, :] = value[:, :128]
            work[8 * i + 2 * j + 1, rows, :] = value[:, 128:]
            return carry

        lax.fori_loop(0, 4, tile, 0)

    def complete(u, names):
        r, half = UNITS[u]
        begin, count = SETS[names[0]][0], 128 * len(names)
        block = 8 * BLOCKS.index((r, 1)) + 4 * half
        for j in range(2):
            columns = slice(512 * half + 256 * j, 512 * half + 256 * j + 256)
            value = jnp.dot(
                other_mixed[begin - 128 : begin - 128 + count, :], weight[SLOT[r], :, columns],
                preferred_element_type=F32,
            )
            rows = pl.ds(begin, count)
            work[block + 2 * j, rows, :] = work[block + 2 * j, rows, :] + value[:, :128]
            work[block + 2 * j + 1, rows, :] = work[block + 2 * j + 1, rows, :] + value[:, 128:]

    def accept(name):
        arrive["z", name].wait_recv()
        at = AS.index(name)
        other_mixed[128 * at : 128 * at + 128, :] = take[at].astype(BF16)

    def add(target, name, source):
        rows = rows_of(name)
        work[target, rows, :] = work[target, rows, :] + source[...]

    def pass_on(name, w, directions=(0, 1)):
        for direction in directions:
            arrive[name, w, 0, direction].wait_recv()
            add(slots((1, 3)[direction], w, direction), name, inbox(name, w, direction))
            ring(name, w, 2, direction)

    def gather(name, w):
        for m in (1, 2):
            for direction in (0, 1):
                arrive[name, w, m, direction].wait_recv()
                half = direction if m == 2 else 1 - direction
                add(slots(0, w, half), name, inbox(name, w, 2 * m + direction))

    writes = []

    def finish(name, box=None):
        rows = rows_of(name)
        for j in range(8):
            value = work[8 * BLOCKS.index((0, 1)) + j, rows, :]
            if box is not None:
                value = value + box[j]
            out_ref[rows, 128 * j : 128 * j + 128] = value.astype(BF16)
        copy = pltpu.make_async_copy(out_ref.at[rows], out_hbm.at[rows], out_sem.at[len(writes)])
        copy.start()
        writes.append(copy)

    gate(0, 0, keep=False)

    def offer(at):
        gate(at + 1, 0)
        arrive["z", AS[at]] = remote(give.at[at], take.at[at], z_send.at[at], z_recv.at[at], across)

    for i in range(8):
        if i > 3:
            weights[i].wait()
        multiply(i, 0, 128)
        own("b", i)
        if i == 3:
            receive(1)
            give_back(3)
            offer(0)
    pair_up(0)
    pair_up(1)
    pass_on("b", 0)
    receive(2)
    offer(1)
    spread(2)
    receive(3)
    spread(3)
    offer(2)
    spread(4)
    give_z(5)
    give_z(6)
    give_z(7)
    for part in returns:
        for copy in part:
            copy.wait_send()
    first0, first1 = fetch(0), fetch(1)
    for i in range(4, 8):
        multiply(i, 128, 384)
    pass_on("b", 1)
    settle(0, first0)
    settle(1, first1)

    def first_step(name):
        accept(name)
        complete(0, [name])
        ring(name, 1, 0, 0)
        complete(1, [name])
        ring(name, 1, 0, 1)

    first_step("a1")
    pair_up(2)
    settle(2, fetch(2))
    complete(2, ["a1"])
    ring("a1", 1, 1, 0)
    gather("b", 0)
    last = remote(work.at[slots(0, 0), rows_of("b"), :], in_zb, z_send.at[3], z_recv.at[3], across)
    first_step("a2")
    complete(2, ["a2"])
    ring("a2", 1, 1, 0)
    pair_up(3)
    settle(3, fetch(3))
    complete(3, ["a1", "a2"])
    ring("a1", 1, 1, 1)
    ring("a2", 1, 1, 1)
    first_step("a3")
    complete(2, ["a3"])
    ring("a3", 1, 1, 0)
    complete(3, ["a3"])
    ring("a3", 1, 1, 1)
    spread(5)
    pair_up(4)
    settle(4, fetch(4))
    complete(4, AS)
    for name in AS:
        pass_on(name, 1, (0,))
    spread(6)
    pair_up(5)
    settle(5, fetch(5))
    complete(5, AS)
    for name in AS:
        pass_on(name, 1, (1,))
    spread(7)
    pair_up(6)
    pair_up(7)
    gather("b", 1)
    last.wait_recv()
    finish("b", in_zb)
    settle(6, fetch(6))
    complete(6, AS)
    settle(7, fetch(7))
    complete(7, AS)
    for name in AS:
        gather(name, 1)
        finish(name)
    for copy in started:
        copy.wait_send()
    for copy in writes:
        copy.wait()


def shards(outer_gate, inner_gate, signal, filter_taps, skip_gain, out_weight):
    vmem = pl.BlockSpec(memory_space=pltpu.VMEM)
    hbm = pl.BlockSpec(memory_space=pl.ANY)
    dma = pltpu.SemaphoreType.DMA
    projected, _ = pl.pallas_call(
        layer_kernel,
        name="layer",
        out_shape=(
            jax.ShapeDtypeStruct((512, 1024), BF16),
            jax.ShapeDtypeStruct((8, 4, 1024, 128), F32),
        ),
        in_specs=[vmem] + [hbm] * 10,
        out_specs=(hbm, hbm),
        scratch_shapes=[
            pltpu.VMEM((64, 512, 128), F32),
            pltpu.VMEM((8, 1024, 1024), BF16),
            pltpu.VMEM((4, 1024, 128), F32),
            pltpu.VMEM((4, 1024, 128), F32),
            pltpu.VMEM((512, 1024), BF16),
            pltpu.VMEM((512, 1024), BF16),
            pltpu.VMEM((512, 1024), BF16),
            pltpu.VMEM((2, 512, 512), BF16),
            pltpu.VMEM((2, 512, 512), BF16),
            pltpu.VMEM((2, 256, 256), BF16),
            pltpu.VMEM((2, 256, 256), BF16),
            pltpu.VMEM((128, 128), F32),
            pltpu.VMEM((2, 6, 4, 128, 128), F32),
            pltpu.VMEM((3, 6, 4, 128, 128), F32),
            pltpu.VMEM((8, 128, 128), F32),
            pltpu.VMEM((3, 128, 1024), F32),
            pltpu.VMEM((3, 128, 1024), F32),
            pltpu.VMEM((384, 1024), BF16),
            pltpu.VMEM((8, 2, 4, 64, 128), F32),
            dma((8, 3)), dma((6,)), dma((8,)), dma((8,)), dma((4,)),
            dma((16,)), dma((16,)), dma((4, 16)), dma((4, 16)),
            dma((5, 6)), dma((5, 6)), dma((4,)), dma((4,)),
            dma((8, 4)), dma((8, 4)), dma((8, 3)), dma((8, 3)), dma((8, 4)), dma((8, 4)),
        ],
        compiler_params=pltpu.CompilerParams(
            collective_id=0, has_side_effects=True, vmem_limit_bytes=62 << 20
        ),
    )(
        skip_gain.reshape(1, -1), inner_gate, signal, filter_taps, outer_gate, out_weight, *tables(),
    )
    return projected


def solution(mesh):
    in_specs = (
        P("ctx", "tp"),
        P("ctx", "tp"),
        P("ctx", "tp"),
        P("ctx", "tp"),
        P("tp"),
        P("tp", None),
    )
    return jax.shard_map(shards, mesh=mesh, in_specs=in_specs, out_specs=P("ctx", "tp"), check_vma=False)
```

```python
import functools
import math

import jax
import jax.numpy as jnp
import numpy as np
from jax import lax
from jax.experimental import pallas as pl
from jax.experimental.pallas import tpu as pltpu
from jax.sharding import PartitionSpec as P

MESH = pl.DeviceIdType.MESH
F32 = jnp.float32
BF16 = jnp.bfloat16

ORDER = ((2, 1), (2, -1), (1, 1), (-1, -1), (1, -1), (-1, 1), (0, 1), (0, -1))
SETS = {"b": (0, 128), "a1": (128, 128), "a2": (256, 128), "a3": (384, 128)}
AS = ("a1", "a2", "a3")
UNITS = ((2, 0), (2, 1), (1, 1), (3, 0), (1, 0), (3, 1), (0, 0), (0, 1))
SLOT = {2: 0, 1: 1, 3: 2, 0: 3}


def split(value):
    high = value.astype(BF16)
    low = (value - high.astype(F32)).astype(BF16)
    return high, low


def split_np(value):
    value = np.asarray(value, np.float64)
    high = value.astype(BF16)
    low = (value - high.astype(np.float64)).astype(BF16)
    return np.stack([high, low])


def tables():
    n1 = np.arange(64)[None, :]
    k1 = np.arange(32)[:, None]
    cos = np.cos(2 * np.pi * (n1 * k1 % 64) / 64)
    sin = np.sin(2 * np.pi * (n1 * k1 % 64) / 64)
    ahead = np.stack([cos, -sin], axis=1)
    ahead[0, 1] = (-1.0) ** np.arange(64)
    ahead = ahead.reshape(64, 64)
    back = np.stack([2 * cos, -2 * sin], axis=1)
    back[0, 0] = 1.0
    back[0, 1] = (-1.0) ** np.arange(64)
    back = back.reshape(64, 64).T / 8192
    back = back.reshape(16, 4, 64).transpose(1, 0, 2).reshape(64, 64)
    eye = np.eye(8)
    n2 = np.arange(128)
    angle = 2 * np.pi * (n2[:, None] * n2[None, :] % 128) / 128
    c, s = np.cos(angle), np.sin(angle)
    fwd = np.block([[c, s], [-s, c]])
    inv = np.block([[c, -s], [s, c]])
    turn = 2 * np.pi * (n2[:, None] * np.arange(33)[None, :]) / 8192
    twist = np.zeros((128, 128))
    twist[:, :33] = np.cos(turn)
    twist[:, 64:97] = np.sin(turn)
    return (
        split_np(np.kron(ahead, eye)),
        split_np(np.kron(back, eye)),
        split_np(fwd),
        split_np(inv),
        twist.astype(np.float32),
    )


def dot3(matrix_ref, value):
    high, low = split(value)
    big, small = matrix_ref[0], matrix_ref[1]
    total = jnp.dot(big, low, preferred_element_type=F32)
    total += jnp.dot(small, high, preferred_element_type=F32)
    return total + jnp.dot(big, high, preferred_element_type=F32)


def here():
    ctx, tp = lax.axis_index("ctx"), lax.axis_index("tp")
    return ctx, tp


SEND, RECV, SPEC, PROD, TAPS = 0, 16, 32, 49, 32
BLOCKS = ((2, 0), (1, 0), (3, 0), (0, 0), (2, 1), (1, 1), (3, 1), (0, 1))


def layer_kernel(
    skip_ref, inner_hbm, signal_hbm, taps_hbm, outer_hbm, weight_hbm,
    ahead_hbm, back_hbm, fwd_hbm, inv_hbm, twist_hbm,
    out_hbm, wide,
    work, weight, result, home, mixed_ref, out_ref,
    outer_ref, ahead_ref, back_ref, fwd_ref, inv_ref, twist_ref,
    in_b, in_a, in_zb, give, take, other_mixed, share,
    in_sem, load_sem, weight_sem, wide_sem, out_sem, out_send, out_recv, back_send, back_recv,
    y_send, y_recv, z_send, z_recv, wz_send, wz_recv, wx_send, wx_recv, wc_send, wc_recv,
):
    ctx, tp = here()
    z_hi, x, core = ctx // 8, (ctx // 2) % 4, ctx % 2
    y, z_lo = tp // 2, tp % 2
    z = 2 * z_hi + z_lo
    partner_tp = tp + 1 - 2 * z_lo
    sign = 1 - 2 * core
    up = (ctx, 2 * ((y + 1) % 4) + z_lo)
    down = (ctx, 2 * ((y + 3) % 4) + z_lo)
    across = (ctx, partner_tp)
    sides = [(8 * ((z + d) % 4 // 2) + 2 * x + core, partner_tp) for d in (1, 3)]
    rights = [(8 * z_hi + 2 * ((x + d) % 4) + core, tp) for d in (1, 3)]
    twin = (ctx + sign, tp)

    quads = []
    for dx, dz in ORDER:
        to_z = (z + dz * sign + 4) % 4
        quads.append((to_z // 2) * 4 + (x + dx * sign + 4) % 4)

    def boxes(begin, count):
        columns = pl.ds(128 * begin, 128 * count)
        return (
            weight.at[7, pl.ds(0, 512), columns], weight.at[7, pl.ds(512, 512), columns],
            work.at[pl.ds(TAPS + begin, count)],
        )

    for step, q in enumerate(quads):
        columns = pl.ds(pl.multiple_of(q * 128, 128), 128)
        near, far, last = boxes(step, 1)
        for i, (src, dst) in enumerate(((inner_hbm, near), (signal_hbm, far), (taps_hbm, last.at[0]))):
            pltpu.make_async_copy(src.at[:, columns], dst, in_sem.at[min(step, 1), i]).start()

    def landed(ref, sem):
        pltpu.make_async_remote_copy(ref, ref, sem, sem, device_id=twin, device_id_type=MESH).wait_recv()

    def departed(ref, sem):
        pltpu.make_async_remote_copy(ref, ref, sem, sem, device_id=twin, device_id_type=MESH).wait_send()

    barrier = pltpu.get_barrier_semaphore()
    for q in quads:
        for k in (0, 1):
            pl.semaphore_signal(barrier, inc=1, device_id=(2 * q + k, partner_tp), device_id_type=MESH)
    for device in [up, down, twin] + rights:
        pl.semaphore_signal(barrier, inc=1, device_id=device, device_id_type=MESH)

    loads = []
    for i, (src, dst) in enumerate(
        (
            (ahead_hbm, ahead_ref), (fwd_hbm, fwd_ref), (inv_hbm, inv_ref),
            (back_hbm, back_ref), (twist_hbm, twist_ref), (outer_hbm, outer_ref),
        )
    ):
        copy = pltpu.make_async_copy(src, dst, load_sem.at[i])
        copy.start()
        loads.append(copy)

    def load_weight(i):
        r, w = BLOCKS[i]
        other = z_lo if w else 1 - z_lo
        start = pl.multiple_of((2 * ((y + r) % 4) + other) * 1024, 1024)
        copy = pltpu.make_async_copy(weight_hbm.at[:, pl.ds(start, 1024)], weight.at[i], weight_sem.at[i])
        copy.start()
        return copy

    weights = [load_weight(i) for i in range(7)]

    lane = lax.broadcasted_iota(jnp.int32, (128, 128), 1)
    first = lane < 64
    row0 = lax.broadcasted_iota(jnp.int32, (128, 128), 0)
    for step, q in enumerate(quads):
        skip = skip_ref[:, pl.ds(pl.multiple_of(q * 128, 128), 128)]
        if step < 2:
            for i, box in enumerate(boxes(step, 1 + 6 * step)):
                pltpu.make_async_copy(box, box, in_sem.at[step, i]).wait()

        def pack(i, carry, step=step, skip=skip, q=q):
            start = pl.multiple_of(i * 128, 128)
            rows = pl.ds(start, 128)
            columns = pl.ds(128 * step, 128)
            gated = weight[7, rows, columns].astype(F32) * weight[7, pl.ds(512 + start, 128), columns].astype(F32)
            taps = work[TAPS + step, rows, :] + jnp.where(row0 + i * 128 + ctx * 512 == 0, skip, 0.0)
            work[SEND + 2 * q, rows, :] = jnp.where(first, gated, pltpu.roll(taps, 64, 1))
            work[SEND + 2 * q + 1, rows, :] = jnp.where(first, pltpu.roll(gated, 64, 1), taps)
            return carry

        lax.fori_loop(0, 4, pack, 0)
        if step == 0:
            pl.semaphore_wait(barrier, 21)
        for dk in (0, 1):
            k = (core + dk) % 2
            copy = pltpu.make_async_remote_copy(
                work.at[SEND + 2 * q + k], work.at[RECV + ctx],
                out_send, out_recv,
                device_id=(2 * q + k, partner_tp), device_id_type=MESH,
            )
            copy.start()
    weights.append(load_weight(7))
    for copy in loads:
        copy.wait()
    mine = pl.multiple_of(256 * x + 128 * core + 64 * z_hi, 64)
    for i in range(4):
        weights[i].wait()
    for u, (r, half) in enumerate(UNITS):
        for c in range(4):
            columns = slice(512 * half + 128 * c, 512 * half + 128 * c + 128)
            share[u, c] = weight[SLOT[r], pl.ds(mine, 64), columns].astype(F32)
    landed(work.at[pl.ds(RECV, 16)], out_recv)

    def remote(src, dst, send_sem, recv_sem, device):
        pltpu.make_async_remote_copy(
            src, dst, send_sem, recv_sem, device_id=device, device_id_type=MESH
        ).start()

    def give_z(u):
        for h in (0, 1):
            remote(share.at[u], wide.at[u, :, pl.ds(mine, 64)], wz_send.at[u], wz_recv.at[u], sides[h])

    def quarter(u, d, begin=0, count=128):
        start = pl.multiple_of(256 * ((x + d) % 4) + 128 * core + begin, 64)
        return wide.at[u, :, pl.ds(start, count)]

    def rows_of_unit(u, count):
        return wide.at[u, :, pl.ds(0, count)]

    def give_core(u, d):
        remote(quarter(u, d), quarter(u, d), wc_send.at[u], wc_recv.at[u], twin)

    def spread(u):
        landed(quarter(u, 0), wz_recv.at[u])
        for n in range(2):
            remote(quarter(u, 0), quarter(u, 0), wx_send.at[u], wx_recv.at[u, 0], rights[n])
        give_core(u, 0)

    def pair_up(u):
        landed(rows_of_unit(u, 256), wx_recv.at[u, 0])
        for n, d in enumerate((3, 1)):
            half = quarter(u, d, 64 * n, 64)
            remote(half, half, wx_send.at[u], wx_recv.at[u, 1], rights[n])
        for d in (3, 1):
            give_core(u, d)

    def close(u):
        landed(quarter(u, 2), wx_recv.at[u, 1])
        give_core(u, 2)

    def fetch(u):
        landed(rows_of_unit(u, 512), wc_recv.at[u])
        copy = pltpu.make_async_copy(wide.at[u], (result, home)[u % 2], wide_sem.at[u % 2])
        copy.start()
        return copy

    def settle(u, copy):
        copy.wait()
        r, half = UNITS[u]
        box = (result, home)[u % 2]

        def convert(i, carry):
            rows = pl.ds(pl.multiple_of(i * 128, 128), 128)
            for c in range(4):
                columns = slice(512 * half + 128 * c, 512 * half + 128 * c + 128)
                weight[SLOT[r], rows, columns] = box[c, rows, :].astype(BF16)
            return carry

        lax.fori_loop(0, 8, convert, 0)

    for u in range(4):
        give_z(u)

    first8 = lax.broadcasted_iota(jnp.int32, (8, 128), 1) < 64

    def put_spec(k1, part, half, a, value):
        start = (k1 % 2) * 256 + part * 128 + half * 64 + a * 8
        work[SPEC + k1 // 2, pl.ds(pl.multiple_of(start, 8), 8), :] = value

    def prod_at(pair, part, rows):
        start = (pair % 2) * 256 + part * 128 + rows
        return work[PROD + pair // 2, pl.ds(pl.multiple_of(start, 8), 8), :]

    def stage_one(a):
        parts = []
        for half in (0, 1):
            start = pl.multiple_of(half * 64 + a * 8, 8)
            parts.append(
                jnp.concatenate(
                    [
                        work[RECV + s, pl.ds(pl.multiple_of(j * 128 + start, 8), 8), :]
                        for s in range(16)
                        for j in range(4)
                    ],
                    axis=0,
                )
            )
        out = dot3(ahead_ref, jnp.concatenate(parts, axis=1))
        for half in (0, 1):
            rows = pl.ds(pl.multiple_of(half * 64 + a * 8, 8), 8)
            twist = twist_ref[rows, :]
            for k1 in range(33):
                if k1 == 0:
                    put_spec(0, 0, half, a, out[0:8, half * 128 : half * 128 + 128])
                    put_spec(0, 1, half, a, jnp.zeros((8, 128), F32))
                    continue
                cos, sin = twist[:, k1 : k1 + 1], twist[:, 64 + k1 : 65 + k1]
                if k1 == 32:
                    real = out[8:16, half * 128 : half * 128 + 128]
                    put_spec(32, 0, half, a, real * cos)
                    put_spec(32, 1, half, a, -(real * sin))
                    continue
                real = out[16 * k1 : 16 * k1 + 8, half * 128 : half * 128 + 128]
                imag = out[16 * k1 + 8 : 16 * k1 + 16, half * 128 : half * 128 + 128]
                put_spec(k1, 0, half, a, real * cos + imag * sin)
                put_spec(k1, 1, half, a, imag * cos - real * sin)

    for a in range(8):
        stage_one(a)

    def product(out, j):
        real, imag = out[:128, 128 * j : 128 * j + 128], out[128:, 128 * j : 128 * j + 128]
        real2, imag2 = pltpu.roll(real, 64, 1), pltpu.roll(imag, 64, 1)
        return jnp.concatenate([real * real2 - imag * imag2, real * imag2 + imag * real2], axis=0)

    first256 = lax.broadcasted_iota(jnp.int32, (256, 128), 1) < 64

    def stage_two(i):
        value = jnp.concatenate([work[SPEC + 2 * i + j // 2, 256 * (j % 2) : 256 * (j % 2) + 256, :] for j in range(4)], axis=1)
        out = dot3(fwd_ref, value)
        pairs = [
            jnp.where(first256, product(out, 2 * j), product(out, 2 * j + 1)) for j in range(2)
        ]
        out = dot3(inv_ref, jnp.concatenate(pairs, axis=1))
        for j in range(2):
            work[PROD + i, 256 * j : 256 * j + 256, :] = out[:, 128 * j : 128 * j + 128]

    for i in range(4):
        stage_two(i)
    spread(0)
    for i in range(4, 8):
        stage_two(i)
    out = dot3(fwd_ref, work[SPEC + 16, 0:256, :])
    work[PROD + 8, 0:256, :] = dot3(inv_ref, product(out, 0))

    def stage_three(a2):
        sides = []
        for side in (0, 1):
            a = 2 * a2 + side
            low = pl.ds(pl.multiple_of(a * 8, 8), 8)
            high = pl.ds(pl.multiple_of(64 + a * 8, 8), 8)
            near, far = twist_ref[low, :], twist_ref[high, :]

            def turn(k1):
                cos = jnp.where(first8, near[:, k1 : k1 + 1], far[:, k1 : k1 + 1])
                sin = jnp.where(first8, near[:, 64 + k1 : 65 + k1], far[:, 64 + k1 : 65 + k1])
                return cos, sin

            pieces = []
            for pair in range(16):
                here_re, here_im = prod_at(pair, 0, a * 8), prod_at(pair, 1, a * 8)
                next_re, next_im = prod_at(pair, 0, 64 + a * 8), prod_at(pair, 1, 64 + a * 8)
                for odd in (0, 1):
                    k1 = 2 * pair + odd
                    if odd:
                        real = jnp.where(first8, pltpu.roll(here_re, 64, 1), next_re)
                        imag = jnp.where(first8, pltpu.roll(here_im, 64, 1), next_im)
                    else:
                        real = jnp.where(first8, here_re, pltpu.roll(next_re, 64, 1))
                        imag = jnp.where(first8, here_im, pltpu.roll(next_im, 64, 1))
                    if k1 == 0:
                        pieces.append(real)
                        real = jnp.where(first8, prod_at(16, 0, a * 8), prod_at(16, 0, 64 + a * 8))
                        imag = jnp.where(first8, prod_at(16, 1, a * 8), prod_at(16, 1, 64 + a * 8))
                        cos, sin = turn(32)
                        pieces.append(real * cos - imag * sin)
                        continue
                    cos, sin = turn(k1)
                    pieces.append(real * cos - imag * sin)
                    pieces.append(real * sin + imag * cos)
            sides.append(jnp.concatenate(pieces, axis=0))
        out = dot3(back_ref, jnp.concatenate(sides, axis=1))
        for side in (0, 1):
            value = out[:, 128 * side : 128 * side + 128].reshape(4, 16, 8, 128)
            for s in range(16):
                result[:, pl.ds(pl.multiple_of(64 * s + (2 * a2 + side) * 8, 8), 8), :] = value[:, s]

    for a2 in range(4):
        stage_three(a2)

    departed(work.at[pl.ds(SEND, 16)], out_send)

    def give_back(part):
        for step, q in enumerate(quads):
            for dk in (0, 1):
                other = 2 * q + (core + dk) % 2
                copy = pltpu.make_async_remote_copy(
                    result.at[part, pl.ds(pl.multiple_of(64 * other, 64), 64)],
                    home.at[part, pl.ds(pl.multiple_of(64 * ctx, 64), 64)],
                    back_send.at[part], back_recv.at[part],
                    device_id=(other, partner_tp), device_id_type=MESH,
                )
                copy.start()

    def receive(part):
        landed(home.at[part], back_recv.at[part])

    give_back(0)
    give_back(1)
    receive(0)
    give_back(2)
    spread(1)
    first64 = lax.broadcasted_iota(jnp.int32, (64, 128), 1) < 64

    def gate(j, carry, keep=True):
        base = pl.multiple_of(j * 128, 128)
        for q in range(8):
            even, odd = home[j, 128 * q : 128 * q + 64, :], home[j, 128 * q + 64 : 128 * q + 128, :]
            for rows, conv in (
                (pl.ds(base, 64), jnp.where(first64, even, pltpu.roll(odd, 64, 1))),
                (pl.ds(base + 64, 64), jnp.where(first64, pltpu.roll(even, 64, 1), odd)),
            ):
                gated = outer_ref[rows, 128 * q : 128 * q + 128].astype(F32) * conv
                rounded = gated.astype(BF16)
                mixed_ref[rows, 128 * q : 128 * q + 128] = rounded
                if keep:
                    begin = 64 * (rows.start != base)
                    give[j - 1, pl.ds(begin, 64), 128 * q : 128 * q + 128] = rounded.astype(F32)
        return carry

    lane_of = {("b", 0): 0, ("b", 1): 1, ("a1", 1): 2, ("a2", 1): 3, ("a3", 1): 4}

    def rows_of(name):
        return pl.ds(*SETS[name])

    def slots(r, w, half=None):
        block = 8 * BLOCKS.index((r, w))
        return pl.ds(block, 8) if half is None else pl.ds(block + 4 * half, 4)

    def inbox(name, w, slot):
        return in_b.at[w, slot] if name == "b" else in_a.at[AS.index(name), slot]

    def ring(name, w, m, direction):
        r = 2 if m == 0 else (1 if direction == 0 else 3)
        half = direction if m in (0, 2) else 1 - direction
        slot = 2 * m + direction
        at = lane_of[name, w]
        remote(
            work.at[slots(r, w, half), rows_of(name), :], inbox(name, w, slot),
            y_send.at[at], y_recv.at[at, min(slot, 2)], up if direction == 0 else down,
        )

    def own(name, i):
        r, w = BLOCKS[i]
        if r == 2:
            ring(name, w, 0, 0)
            ring(name, w, 0, 1)
        elif r == 1:
            ring(name, w, 1, 0)
        elif r == 3:
            ring(name, w, 1, 1)

    def multiply(i, begin, count):
        def tile(j, carry):
            columns = pl.ds(pl.multiple_of(j * 256, 256), 256)
            rows = pl.ds(begin, count)
            value = jnp.dot(mixed_ref[rows, :], weight[i, :, columns], preferred_element_type=F32)
            work[8 * i + 2 * j, rows, :] = value[:, :128]
            work[8 * i + 2 * j + 1, rows, :] = value[:, 128:]
            return carry

        lax.fori_loop(0, 4, tile, 0)

    def complete(u, names):
        r, half = UNITS[u]
        begin, count = SETS[names[0]][0], 128 * len(names)
        block = 8 * BLOCKS.index((r, 1)) + 4 * half
        for j in range(2):
            columns = slice(512 * half + 256 * j, 512 * half + 256 * j + 256)
            value = jnp.dot(
                other_mixed[begin - 128 : begin - 128 + count, :], weight[SLOT[r], :, columns],
                preferred_element_type=F32,
            )
            rows = pl.ds(begin, count)
            work[block + 2 * j, rows, :] = work[block + 2 * j, rows, :] + value[:, :128]
            work[block + 2 * j + 1, rows, :] = work[block + 2 * j + 1, rows, :] + value[:, 128:]

    def accept(name):
        at = AS.index(name)
        landed(take.at[at], z_recv.at[at])
        other_mixed[128 * at : 128 * at + 128, :] = take[at].astype(BF16)

    def add(target, name, source):
        rows = rows_of(name)
        work[target, rows, :] = work[target, rows, :] + source[...]

    def pass_on(name, w, directions=(0, 1)):
        for direction in directions:
            landed(inbox(name, w, direction), y_recv.at[lane_of[name, w], direction])
            add(slots((1, 3)[direction], w, direction), name, inbox(name, w, direction))
            ring(name, w, 2, direction)

    def box_of(name, w):
        return in_b.at[w] if name == "b" else in_a.at[AS.index(name)]

    def gather(name, w):
        landed(box_of(name, w).at[pl.ds(2, 4)], y_recv.at[lane_of[name, w], 2])
        for m in (1, 2):
            for direction in (0, 1):
                half = direction if m == 2 else 1 - direction
                add(slots(0, w, half), name, inbox(name, w, 2 * m + direction))

    writes = []

    def finish(name, box=None):
        rows = rows_of(name)
        for j in range(8):
            value = work[8 * BLOCKS.index((0, 1)) + j, rows, :]
            if box is not None:
                value = value + box[j]
            out_ref[rows, 128 * j : 128 * j + 128] = value.astype(BF16)
        copy = pltpu.make_async_copy(out_ref.at[rows], out_hbm.at[rows], out_sem.at[len(writes)])
        copy.start()
        writes.append(copy)

    gate(0, 0, keep=False)

    def offer(at):
        gate(at + 1, 0)
        remote(give.at[at], take.at[at], z_send.at[0], z_recv.at[at], across)

    for i in range(8):
        if i > 3:
            weights[i].wait()
        multiply(i, 0, 128)
        own("b", i)
        if i == 3:
            receive(1)
            give_back(3)
            offer(0)
            give_z(4)
    pair_up(0)
    pass_on("b", 0)
    receive(2)
    offer(1)
    give_z(5)
    spread(2)
    pair_up(1)
    receive(3)
    spread(3)
    offer(2)
    pass_on("b", 1)
    give_z(6)
    give_z(7)
    for part in range(4):
        departed(result.at[part], back_send.at[part])
    multiply(4, 128, 384)
    close(0)
    multiply(5, 128, 384)
    close(1)
    first0 = fetch(0)
    multiply(6, 128, 384)
    pair_up(2)
    settle(0, first0)

    def first_step(name):
        accept(name)
        complete(0, [name])
        ring(name, 1, 0, 0)
        complete(1, [name])
        ring(name, 1, 0, 1)

    accept("a1")
    complete(0, ["a1"])
    ring("a1", 1, 0, 0)
    first1 = fetch(1)
    multiply(7, 128, 384)
    settle(1, first1)
    complete(1, ["a1"])
    ring("a1", 1, 0, 1)
    pair_up(3)
    spread(4)
    first_step("a2")
    close(2)
    settle(2, fetch(2))
    complete(2, ["a1", "a2"])
    ring("a1", 1, 1, 0)
    ring("a2", 1, 1, 0)
    gather("b", 0)
    remote(work.at[slots(0, 0), rows_of("b"), :], in_zb, z_send.at[1], z_recv.at[3], across)
    spread(5)
    close(3)
    settle(3, fetch(3))
    complete(3, ["a1", "a2"])
    ring("a1", 1, 1, 1)
    ring("a2", 1, 1, 1)
    pair_up(4)
    first_step("a3")
    complete(2, ["a3"])
    ring("a3", 1, 1, 0)
    complete(3, ["a3"])
    ring("a3", 1, 1, 1)
    close(4)
    pair_up(5)
    settle(4, fetch(4))
    complete(4, AS)
    spread(6)
    for name in AS[:2]:
        pass_on(name, 1, (0,))
    close(5)
    settle(5, fetch(5))
    complete(5, AS)
    spread(7)
    for name in AS[:2]:
        pass_on(name, 1, (1,))
    pair_up(6)
    pass_on("a3", 1)
    pair_up(7)
    gather("b", 1)
    landed(in_zb, z_recv.at[3])
    finish("b", in_zb)
    for u in (6, 7):
        close(u)
        settle(u, fetch(u))
        complete(u, AS)
    for name in AS:
        gather(name, 1)
        finish(name)
    for u in range(8):
        departed(rows_of_unit(u, 128), wz_send.at[u])
        departed(rows_of_unit(u, 384), wx_send.at[u])
        departed(rows_of_unit(u, 512), wc_send.at[u])
    for (name, w), at in lane_of.items():
        departed(box_of(name, w), y_send.at[at])
    departed(give, z_send.at[0])
    departed(in_zb, z_send.at[1])
    for copy in writes:
        copy.wait()


def shards(outer_gate, inner_gate, signal, filter_taps, skip_gain, out_weight):
    vmem = pl.BlockSpec(memory_space=pltpu.VMEM)
    hbm = pl.BlockSpec(memory_space=pl.ANY)
    dma = pltpu.SemaphoreType.DMA
    projected, _ = pl.pallas_call(
        layer_kernel,
        name="layer",
        out_shape=(
            jax.ShapeDtypeStruct((512, 1024), BF16),
            jax.ShapeDtypeStruct((8, 4, 1024, 128), F32),
        ),
        in_specs=[vmem] + [hbm] * 10,
        out_specs=(hbm, hbm),
        scratch_shapes=[
            pltpu.VMEM((64, 512, 128), F32),
            pltpu.VMEM((8, 1024, 1024), BF16),
            pltpu.VMEM((4, 1024, 128), F32),
            pltpu.VMEM((4, 1024, 128), F32),
            pltpu.VMEM((512, 1024), BF16),
            pltpu.VMEM((512, 1024), BF16),
            pltpu.VMEM((512, 1024), BF16),
            pltpu.VMEM((2, 512, 512), BF16),
            pltpu.VMEM((2, 512, 512), BF16),
            pltpu.VMEM((2, 256, 256), BF16),
            pltpu.VMEM((2, 256, 256), BF16),
            pltpu.VMEM((128, 128), F32),
            pltpu.VMEM((2, 6, 4, 128, 128), F32),
            pltpu.VMEM((3, 6, 4, 128, 128), F32),
            pltpu.VMEM((8, 128, 128), F32),
            pltpu.VMEM((3, 128, 1024), F32),
            pltpu.VMEM((3, 128, 1024), F32),
            pltpu.VMEM((384, 1024), BF16),
            pltpu.VMEM((8, 4, 64, 128), F32),
            dma((2, 3)), dma((6,)), dma((8,)), dma((2,)), dma((4,)),
            dma, dma, dma((4,)), dma((4,)),
            dma((5,)), dma((5, 3)), dma((2,)), dma((4,)),
            dma((8,)), dma((8,)), dma((8,)), dma((8, 2)), dma((8,)), dma((8,)),
        ],
        compiler_params=pltpu.CompilerParams(
            collective_id=0, has_side_effects=True, vmem_limit_bytes=62 << 20
        ),
    )(
        skip_gain.reshape(1, -1), inner_gate, signal, filter_taps, outer_gate, out_weight, *tables(),
    )
    return projected


def solution(mesh):
    in_specs = (
        P("ctx", "tp"),
        P("ctx", "tp"),
        P("ctx", "tp"),
        P("ctx", "tp"),
        P("tp"),
        P("tp", None),
    )
    return jax.shard_map(shards, mesh=mesh, in_specs=in_specs, out_specs=P("ctx", "tp"), check_vma=False)
```

```python
import functools
import math

import jax
import jax.numpy as jnp
import numpy as np
from jax import lax
from jax.experimental import pallas as pl
from jax.experimental.pallas import tpu as pltpu
from jax.sharding import PartitionSpec as P

MESH = pl.DeviceIdType.MESH
F32 = jnp.float32
BF16 = jnp.bfloat16

ORDER = ((2, 1), (2, -1), (1, 1), (-1, -1), (1, -1), (-1, 1), (0, 1), (0, -1))
SETS = {"b": (0, 128), "a1": (128, 128), "a2": (256, 128), "a3": (384, 128)}
AS = ("a1", "a2", "a3")
UNITS = ((2, 0), (2, 1), (1, 1), (3, 0), (1, 0), (3, 1), (0, 0), (0, 1))
SLOT = {2: 0, 1: 1, 3: 2, 0: 3}


def split(value):
    high = value.astype(BF16)
    low = (value - high.astype(F32)).astype(BF16)
    return high, low


def split_np(value):
    value = np.asarray(value, np.float64)
    high = value.astype(BF16)
    low = (value - high.astype(np.float64)).astype(BF16)
    return np.stack([high, low])


def tables():
    n1 = np.arange(64)[None, :]
    k1 = np.arange(32)[:, None]
    cos = np.cos(2 * np.pi * (n1 * k1 % 64) / 64)
    sin = np.sin(2 * np.pi * (n1 * k1 % 64) / 64)
    ahead = np.stack([cos, -sin], axis=1)
    ahead[0, 1] = (-1.0) ** np.arange(64)
    ahead = ahead.reshape(64, 64)
    back = np.stack([2 * cos, -2 * sin], axis=1)
    back[0, 0] = 1.0
    back[0, 1] = (-1.0) ** np.arange(64)
    back = back.reshape(64, 64).T / 8192
    back = back.reshape(16, 4, 64).transpose(1, 0, 2).reshape(64, 64)
    eye = np.eye(8)
    n2 = np.arange(128)
    angle = 2 * np.pi * (n2[:, None] * n2[None, :] % 128) / 128
    c, s = np.cos(angle), np.sin(angle)
    fwd = np.block([[c, s], [-s, c]])
    inv = np.block([[c, -s], [s, c]])
    turn = 2 * np.pi * (n2[:, None] * np.arange(33)[None, :]) / 8192
    twist = np.zeros((128, 128))
    twist[:, :33] = np.cos(turn)
    twist[:, 64:97] = np.sin(turn)
    return (
        split_np(np.kron(ahead, eye)),
        split_np(np.kron(back, eye)),
        split_np(fwd),
        split_np(inv),
        twist.astype(np.float32),
    )


def dot3(matrix_ref, value):
    high, low = split(value)
    big, small = matrix_ref[0], matrix_ref[1]
    total = jnp.dot(big, low, preferred_element_type=F32)
    total += jnp.dot(small, high, preferred_element_type=F32)
    return total + jnp.dot(big, high, preferred_element_type=F32)


def here():
    ctx, tp = lax.axis_index("ctx"), lax.axis_index("tp")
    return ctx, tp


SEND, RECV, SPEC, PROD, TAPS = 0, 16, 32, 49, 32
BLOCKS = ((2, 0), (1, 0), (3, 0), (0, 0), (2, 1), (1, 1), (3, 1), (0, 1))


def layer_kernel(
    skip_ref, inner_hbm, signal_hbm, taps_hbm, outer_hbm, weight_hbm,
    ahead_hbm, back_hbm, fwd_hbm, inv_hbm, twist_hbm,
    out_hbm, wide,
    work, weight, result, home, mixed_ref, out_ref,
    outer_ref, ahead_ref, back_ref, fwd_ref, inv_ref, twist_ref,
    in_b, in_a, in_zb, give, take, other_mixed, share,
    in_sem, load_sem, weight_sem, wide_sem, out_sem, out_send, out_recv, back_send, back_recv,
    y_send, y_recv, z_send, z_recv, wz_send, wz_recv, wx_send, wx_recv, wc_send, wc_recv,
):
    ctx, tp = here()
    z_hi, x, core = ctx // 8, (ctx // 2) % 4, ctx % 2
    y, z_lo = tp // 2, tp % 2
    z = 2 * z_hi + z_lo
    partner_tp = tp + 1 - 2 * z_lo
    sign = 1 - 2 * core
    up = (ctx, 2 * ((y + 1) % 4) + z_lo)
    down = (ctx, 2 * ((y + 3) % 4) + z_lo)
    across = (ctx, partner_tp)
    sides = [(8 * ((z + d) % 4 // 2) + 2 * x + core, partner_tp) for d in (1, 3)]
    rights = [(8 * z_hi + 2 * ((x + d) % 4) + core, tp) for d in (1, 3)]
    twin = (ctx + sign, tp)

    quads = []
    for dx, dz in ORDER:
        to_z = (z + dz * sign + 4) % 4
        quads.append((to_z // 2) * 4 + (x + dx * sign + 4) % 4)

    def boxes(begin, count):
        columns = pl.ds(128 * begin, 128 * count)
        return (
            weight.at[7, pl.ds(0, 512), columns], weight.at[7, pl.ds(512, 512), columns],
            work.at[pl.ds(TAPS + begin, count)],
        )

    for step, q in enumerate(quads):
        columns = pl.ds(pl.multiple_of(q * 128, 128), 128)
        near, far, last = boxes(step, 1)
        for i, (src, dst) in enumerate(((inner_hbm, near), (signal_hbm, far), (taps_hbm, last.at[0]))):
            pltpu.make_async_copy(src.at[:, columns], dst, in_sem.at[min(step, 1), i]).start()

    def landed(ref, sem):
        pltpu.make_async_remote_copy(ref, ref, sem, sem, device_id=twin, device_id_type=MESH).wait_recv()

    def departed(ref, sem):
        pltpu.make_async_remote_copy(ref, ref, sem, sem, device_id=twin, device_id_type=MESH).wait_send()

    barrier = pltpu.get_barrier_semaphore()
    for q in quads:
        for k in (0, 1):
            pl.semaphore_signal(barrier, inc=1, device_id=(2 * q + k, partner_tp), device_id_type=MESH)
    for device in [up, down, twin] + rights:
        pl.semaphore_signal(barrier, inc=1, device_id=device, device_id_type=MESH)

    loads = []
    for i, (src, dst) in enumerate(
        (
            (ahead_hbm, ahead_ref), (fwd_hbm, fwd_ref), (inv_hbm, inv_ref),
            (back_hbm, back_ref), (twist_hbm, twist_ref), (outer_hbm, outer_ref),
        )
    ):
        copy = pltpu.make_async_copy(src, dst, load_sem.at[i])
        copy.start()
        loads.append(copy)

    def load_weight(i):
        r, w = BLOCKS[i]
        other = z_lo if w else 1 - z_lo
        start = pl.multiple_of((2 * ((y + r) % 4) + other) * 1024, 1024)
        copy = pltpu.make_async_copy(weight_hbm.at[:, pl.ds(start, 1024)], weight.at[i], weight_sem.at[i])
        copy.start()
        return copy

    weights = [load_weight(i) for i in range(7)]

    lane = lax.broadcasted_iota(jnp.int32, (128, 128), 1)
    first = lane < 64
    row0 = lax.broadcasted_iota(jnp.int32, (128, 128), 0)
    for step, q in enumerate(quads):
        skip = skip_ref[:, pl.ds(pl.multiple_of(q * 128, 128), 128)]
        if step < 2:
            for i, box in enumerate(boxes(step, 1 + 6 * step)):
                pltpu.make_async_copy(box, box, in_sem.at[step, i]).wait()

        def pack(i, carry, step=step, skip=skip, q=q):
            start = pl.multiple_of(i * 128, 128)
            rows = pl.ds(start, 128)
            columns = pl.ds(128 * step, 128)
            gated = weight[7, rows, columns].astype(F32) * weight[7, pl.ds(512 + start, 128), columns].astype(F32)
            taps = work[TAPS + step, rows, :] + jnp.where(row0 + i * 128 + ctx * 512 == 0, skip, 0.0)
            work[SEND + 2 * q, rows, :] = jnp.where(first, gated, pltpu.roll(taps, 64, 1))
            work[SEND + 2 * q + 1, rows, :] = jnp.where(first, pltpu.roll(gated, 64, 1), taps)
            return carry

        lax.fori_loop(0, 4, pack, 0)
        if step == 0:
            pl.semaphore_wait(barrier, 21)
        for dk in (0, 1):
            k = (core + dk) % 2
            copy = pltpu.make_async_remote_copy(
                work.at[SEND + 2 * q + k], work.at[RECV + ctx],
                out_send, out_recv,
                device_id=(2 * q + k, partner_tp), device_id_type=MESH,
            )
            copy.start()
    weights.append(load_weight(7))
    for copy in loads:
        copy.wait()
    mine = pl.multiple_of(256 * x + 128 * core + 64 * z_hi, 64)
    for i in range(4):
        weights[i].wait()
    for u, (r, half) in enumerate(UNITS):
        for c in range(4):
            columns = slice(512 * half + 128 * c, 512 * half + 128 * c + 128)
            share[u, c] = weight[SLOT[r], pl.ds(mine, 64), columns].astype(F32)
    landed(work.at[pl.ds(RECV, 16)], out_recv)

    def remote(src, dst, send_sem, recv_sem, device):
        pltpu.make_async_remote_copy(
            src, dst, send_sem, recv_sem, device_id=device, device_id_type=MESH
        ).start()

    def give_z(u):
        for h in (0, 1):
            remote(share.at[u], wide.at[u, :, pl.ds(mine, 64)], wz_send.at[u], wz_recv.at[u], sides[h])

    def quarter(u, d, begin=0, count=128):
        start = pl.multiple_of(256 * ((x + d) % 4) + 128 * core + begin, 64)
        return wide.at[u, :, pl.ds(start, count)]

    def rows_of_unit(u, count):
        return wide.at[u, :, pl.ds(0, count)]

    def give_core(u, d):
        remote(quarter(u, d), quarter(u, d), wc_send.at[u], wc_recv.at[u], twin)

    def spread(u):
        landed(quarter(u, 0), wz_recv.at[u])
        for n in range(2):
            remote(quarter(u, 0), quarter(u, 0), wx_send.at[u], wx_recv.at[u, 0], rights[n])
        give_core(u, 0)

    def pair_up(u):
        landed(rows_of_unit(u, 256), wx_recv.at[u, 0])
        for n, d in enumerate((3, 1)):
            half = quarter(u, d, 64 * n, 64)
            remote(half, half, wx_send.at[u], wx_recv.at[u, 1], rights[n])
        for d in (3, 1):
            give_core(u, d)

    def close(u):
        landed(quarter(u, 2), wx_recv.at[u, 1])
        give_core(u, 2)

    def fetch(u):
        landed(rows_of_unit(u, 512), wc_recv.at[u])
        copy = pltpu.make_async_copy(wide.at[u], (result, home)[u % 2], wide_sem.at[u % 2])
        copy.start()
        return copy

    def settle(u, copy):
        copy.wait()
        r, half = UNITS[u]
        box = (result, home)[u % 2]

        def convert(i, carry):
            rows = pl.ds(pl.multiple_of(i * 128, 128), 128)
            for c in range(4):
                columns = slice(512 * half + 128 * c, 512 * half + 128 * c + 128)
                weight[SLOT[r], rows, columns] = box[c, rows, :].astype(BF16)
            return carry

        lax.fori_loop(0, 8, convert, 0)

    for u in range(4):
        give_z(u)

    first8 = lax.broadcasted_iota(jnp.int32, (8, 128), 1) < 64

    def put_spec(k1, part, half, a, value):
        start = (k1 % 2) * 256 + part * 128 + half * 64 + a * 8
        work[SPEC + k1 // 2, pl.ds(pl.multiple_of(start, 8), 8), :] = value

    def prod_at(pair, part, rows):
        start = (pair % 2) * 256 + part * 128 + rows
        return work[PROD + pair // 2, pl.ds(pl.multiple_of(start, 8), 8), :]

    def stage_one(a):
        parts = []
        for half in (0, 1):
            start = pl.multiple_of(half * 64 + a * 8, 8)
            parts.append(
                jnp.concatenate(
                    [
                        work[RECV + s, pl.ds(pl.multiple_of(j * 128 + start, 8), 8), :]
                        for s in range(16)
                        for j in range(4)
                    ],
                    axis=0,
                )
            )
        out = dot3(ahead_ref, jnp.concatenate(parts, axis=1))
        for half in (0, 1):
            rows = pl.ds(pl.multiple_of(half * 64 + a * 8, 8), 8)
            twist = twist_ref[rows, :]
            for k1 in range(33):
                if k1 == 0:
                    put_spec(0, 0, half, a, out[0:8, half * 128 : half * 128 + 128])
                    put_spec(0, 1, half, a, jnp.zeros((8, 128), F32))
                    continue
                cos, sin = twist[:, k1 : k1 + 1], twist[:, 64 + k1 : 65 + k1]
                if k1 == 32:
                    real = out[8:16, half * 128 : half * 128 + 128]
                    put_spec(32, 0, half, a, real * cos)
                    put_spec(32, 1, half, a, -(real * sin))
                    continue
                real = out[16 * k1 : 16 * k1 + 8, half * 128 : half * 128 + 128]
                imag = out[16 * k1 + 8 : 16 * k1 + 16, half * 128 : half * 128 + 128]
                put_spec(k1, 0, half, a, real * cos + imag * sin)
                put_spec(k1, 1, half, a, imag * cos - real * sin)

    for a in range(8):
        stage_one(a)

    def product(out, j):
        real, imag = out[:128, 128 * j : 128 * j + 128], out[128:, 128 * j : 128 * j + 128]
        real2, imag2 = pltpu.roll(real, 64, 1), pltpu.roll(imag, 64, 1)
        return jnp.concatenate([real * real2 - imag * imag2, real * imag2 + imag * real2], axis=0)

    first256 = lax.broadcasted_iota(jnp.int32, (256, 128), 1) < 64

    def stage_two(i):
        value = jnp.concatenate([work[SPEC + 2 * i + j // 2, 256 * (j % 2) : 256 * (j % 2) + 256, :] for j in range(4)], axis=1)
        out = dot3(fwd_ref, value)
        pairs = [
            jnp.where(first256, product(out, 2 * j), product(out, 2 * j + 1)) for j in range(2)
        ]
        out = dot3(inv_ref, jnp.concatenate(pairs, axis=1))
        for j in range(2):
            work[PROD + i, 256 * j : 256 * j + 256, :] = out[:, 128 * j : 128 * j + 128]

    for i in range(4):
        stage_two(i)
    spread(0)
    for i in range(4, 8):
        stage_two(i)
    out = dot3(fwd_ref, work[SPEC + 16, 0:256, :])
    work[PROD + 8, 0:256, :] = dot3(inv_ref, product(out, 0))

    def stage_three(a2):
        sides = []
        for side in (0, 1):
            a = 2 * a2 + side
            low = pl.ds(pl.multiple_of(a * 8, 8), 8)
            high = pl.ds(pl.multiple_of(64 + a * 8, 8), 8)
            near, far = twist_ref[low, :], twist_ref[high, :]

            def turn(k1):
                cos = jnp.where(first8, near[:, k1 : k1 + 1], far[:, k1 : k1 + 1])
                sin = jnp.where(first8, near[:, 64 + k1 : 65 + k1], far[:, 64 + k1 : 65 + k1])
                return cos, sin

            pieces = []
            for pair in range(16):
                here_re, here_im = prod_at(pair, 0, a * 8), prod_at(pair, 1, a * 8)
                next_re, next_im = prod_at(pair, 0, 64 + a * 8), prod_at(pair, 1, 64 + a * 8)
                for odd in (0, 1):
                    k1 = 2 * pair + odd
                    if odd:
                        real = jnp.where(first8, pltpu.roll(here_re, 64, 1), next_re)
                        imag = jnp.where(first8, pltpu.roll(here_im, 64, 1), next_im)
                    else:
                        real = jnp.where(first8, here_re, pltpu.roll(next_re, 64, 1))
                        imag = jnp.where(first8, here_im, pltpu.roll(next_im, 64, 1))
                    if k1 == 0:
                        pieces.append(real)
                        real = jnp.where(first8, prod_at(16, 0, a * 8), prod_at(16, 0, 64 + a * 8))
                        imag = jnp.where(first8, prod_at(16, 1, a * 8), prod_at(16, 1, 64 + a * 8))
                        cos, sin = turn(32)
                        pieces.append(real * cos - imag * sin)
                        continue
                    cos, sin = turn(k1)
                    pieces.append(real * cos - imag * sin)
                    pieces.append(real * sin + imag * cos)
            sides.append(jnp.concatenate(pieces, axis=0))
        out = dot3(back_ref, jnp.concatenate(sides, axis=1))
        for side in (0, 1):
            value = out[:, 128 * side : 128 * side + 128].reshape(4, 16, 8, 128)
            for s in range(16):
                result[:, pl.ds(pl.multiple_of(64 * s + (2 * a2 + side) * 8, 8), 8), :] = value[:, s]

    for a2 in range(4):
        stage_three(a2)

    departed(work.at[pl.ds(SEND, 16)], out_send)

    def give_back(part):
        for step, q in enumerate(quads):
            for dk in (0, 1):
                other = 2 * q + (core + dk) % 2
                copy = pltpu.make_async_remote_copy(
                    result.at[part, pl.ds(pl.multiple_of(64 * other, 64), 64)],
                    home.at[part, pl.ds(pl.multiple_of(64 * ctx, 64), 64)],
                    back_send.at[part], back_recv.at[part],
                    device_id=(other, partner_tp), device_id_type=MESH,
                )
                copy.start()

    def receive(part):
        landed(home.at[part], back_recv.at[part])

    give_back(0)
    give_back(1)
    receive(0)
    give_back(2)
    first64 = lax.broadcasted_iota(jnp.int32, (64, 128), 1) < 64

    def gate(j, carry, keep=True):
        base = pl.multiple_of(j * 128, 128)
        for q in range(8):
            even, odd = home[j, 128 * q : 128 * q + 64, :], home[j, 128 * q + 64 : 128 * q + 128, :]
            for rows, conv in (
                (pl.ds(base, 64), jnp.where(first64, even, pltpu.roll(odd, 64, 1))),
                (pl.ds(base + 64, 64), jnp.where(first64, pltpu.roll(even, 64, 1), odd)),
            ):
                gated = outer_ref[rows, 128 * q : 128 * q + 128].astype(F32) * conv
                rounded = gated.astype(BF16)
                mixed_ref[rows, 128 * q : 128 * q + 128] = rounded
                if keep:
                    begin = 64 * (rows.start != base)
                    give[j - 1, pl.ds(begin, 64), 128 * q : 128 * q + 128] = rounded.astype(F32)
        return carry

    lane_of = {("b", 0): 0, ("b", 1): 1, ("a1", 1): 2, ("a2", 1): 3, ("a3", 1): 4}

    def rows_of(name):
        return pl.ds(*SETS[name])

    def slots(r, w, half=None):
        block = 8 * BLOCKS.index((r, w))
        return pl.ds(block, 8) if half is None else pl.ds(block + 4 * half, 4)

    def inbox(name, w, slot):
        return in_b.at[w, slot] if name == "b" else in_a.at[AS.index(name), slot]

    def ring(name, w, m, direction):
        r = 2 if m == 0 else (1 if direction == 0 else 3)
        half = direction if m in (0, 2) else 1 - direction
        slot = 2 * m + direction
        at = lane_of[name, w]
        remote(
            work.at[slots(r, w, half), rows_of(name), :], inbox(name, w, slot),
            y_send.at[at], y_recv.at[at, min(slot, 2)], up if direction == 0 else down,
        )

    def own(name, i):
        r, w = BLOCKS[i]
        if r == 2:
            ring(name, w, 0, 0)
            ring(name, w, 0, 1)
        elif r == 1:
            ring(name, w, 1, 0)
        elif r == 3:
            ring(name, w, 1, 1)

    def multiply(i, begin, count):
        def tile(j, carry):
            columns = pl.ds(pl.multiple_of(j * 256, 256), 256)
            rows = pl.ds(begin, count)
            value = jnp.dot(mixed_ref[rows, :], weight[i, :, columns], preferred_element_type=F32)
            work[8 * i + 2 * j, rows, :] = value[:, :128]
            work[8 * i + 2 * j + 1, rows, :] = value[:, 128:]
            return carry

        lax.fori_loop(0, 4, tile, 0)

    def complete(u, names):
        r, half = UNITS[u]
        begin, count = SETS[names[0]][0], 128 * len(names)
        block = 8 * BLOCKS.index((r, 1)) + 4 * half
        for j in range(2):
            columns = slice(512 * half + 256 * j, 512 * half + 256 * j + 256)
            value = jnp.dot(
                other_mixed[begin - 128 : begin - 128 + count, :], weight[SLOT[r], :, columns],
                preferred_element_type=F32,
            )
            rows = pl.ds(begin, count)
            work[block + 2 * j, rows, :] = work[block + 2 * j, rows, :] + value[:, :128]
            work[block + 2 * j + 1, rows, :] = work[block + 2 * j + 1, rows, :] + value[:, 128:]

    def accept(name):
        at = AS.index(name)
        landed(take.at[at], z_recv.at[at])
        other_mixed[128 * at : 128 * at + 128, :] = take[at].astype(BF16)

    def add(target, name, source):
        rows = rows_of(name)
        work[target, rows, :] = work[target, rows, :] + source[...]

    def pass_on(name, w, directions=(0, 1)):
        for direction in directions:
            landed(inbox(name, w, direction), y_recv.at[lane_of[name, w], direction])
            add(slots((1, 3)[direction], w, direction), name, inbox(name, w, direction))
            ring(name, w, 2, direction)

    def box_of(name, w):
        return in_b.at[w] if name == "b" else in_a.at[AS.index(name)]

    def gather(name, w):
        landed(box_of(name, w).at[pl.ds(2, 4)], y_recv.at[lane_of[name, w], 2])
        for m in (1, 2):
            for direction in (0, 1):
                half = direction if m == 2 else 1 - direction
                add(slots(0, w, half), name, inbox(name, w, 2 * m + direction))

    writes = []

    def finish(name, box=None):
        rows = rows_of(name)
        for j in range(8):
            value = work[8 * BLOCKS.index((0, 1)) + j, rows, :]
            if box is not None:
                value = value + box[j]
            out_ref[rows, 128 * j : 128 * j + 128] = value.astype(BF16)
        copy = pltpu.make_async_copy(out_ref.at[rows], out_hbm.at[rows], out_sem.at[len(writes)])
        copy.start()
        writes.append(copy)

    gate(0, 0, keep=False)

    def offer(at):
        gate(at + 1, 0)
        remote(give.at[at], take.at[at], z_send.at[0], z_recv.at[at], across)

    for i in range(8):
        if i > 3:
            weights[i].wait()
        multiply(i, 0, 128)
        own("b", i)
        if i == 3:
            receive(1)
            give_back(3)
            offer(0)
            pair_up(0)
            spread(1)
    pass_on("b", 0)
    receive(2)
    offer(1)
    give_z(4)
    give_z(5)
    spread(2)
    receive(3)
    offer(2)
    give_z(6)
    give_z(7)
    for part in range(4):
        departed(result.at[part], back_send.at[part])
    multiply(4, 128, 384)
    close(0)
    first0 = fetch(0)
    multiply(5, 128, 384)
    pass_on("b", 1)
    pair_up(1)
    spread(3)
    multiply(6, 128, 384)
    settle(0, first0)

    def first_step(name):
        accept(name)
        complete(0, [name])
        ring(name, 1, 0, 0)
        complete(1, [name])
        ring(name, 1, 0, 1)

    accept("a1")
    complete(0, ["a1"])
    ring("a1", 1, 0, 0)
    pair_up(2)
    close(1)
    first1 = fetch(1)
    multiply(7, 128, 384)
    settle(1, first1)
    complete(1, ["a1"])
    ring("a1", 1, 0, 1)
    pair_up(3)
    first_step("a2")
    spread(4)
    close(2)
    settle(2, fetch(2))
    complete(2, ["a1", "a2"])
    ring("a1", 1, 1, 0)
    ring("a2", 1, 1, 0)
    gather("b", 0)
    remote(work.at[slots(0, 0), rows_of("b"), :], in_zb, z_send.at[1], z_recv.at[3], across)
    spread(5)
    close(3)
    settle(3, fetch(3))
    complete(3, ["a1", "a2"])
    ring("a1", 1, 1, 1)
    ring("a2", 1, 1, 1)
    pair_up(4)
    first_step("a3")
    complete(2, ["a3"])
    ring("a3", 1, 1, 0)
    complete(3, ["a3"])
    ring("a3", 1, 1, 1)
    close(4)
    pair_up(5)
    settle(4, fetch(4))
    complete(4, AS)
    spread(6)
    for name in AS[:2]:
        pass_on(name, 1, (0,))
    close(5)
    settle(5, fetch(5))
    complete(5, AS)
    spread(7)
    for name in AS[:2]:
        pass_on(name, 1, (1,))
    pair_up(6)
    pass_on("a3", 1)
    pair_up(7)
    gather("b", 1)
    landed(in_zb, z_recv.at[3])
    finish("b", in_zb)
    for u in (6, 7):
        close(u)
        settle(u, fetch(u))
        complete(u, AS)
    for name in AS:
        gather(name, 1)
        finish(name)
    for u in range(8):
        departed(rows_of_unit(u, 128), wz_send.at[u])
        departed(rows_of_unit(u, 384), wx_send.at[u])
        departed(rows_of_unit(u, 512), wc_send.at[u])
    for (name, w), at in lane_of.items():
        departed(box_of(name, w), y_send.at[at])
    departed(give, z_send.at[0])
    departed(in_zb, z_send.at[1])
    for copy in writes:
        copy.wait()


def shards(outer_gate, inner_gate, signal, filter_taps, skip_gain, out_weight):
    vmem = pl.BlockSpec(memory_space=pltpu.VMEM)
    hbm = pl.BlockSpec(memory_space=pl.ANY)
    dma = pltpu.SemaphoreType.DMA
    projected, _ = pl.pallas_call(
        layer_kernel,
        name="layer",
        out_shape=(
            jax.ShapeDtypeStruct((512, 1024), BF16),
            jax.ShapeDtypeStruct((8, 4, 1024, 128), F32),
        ),
        in_specs=[vmem] + [hbm] * 10,
        out_specs=(hbm, hbm),
        scratch_shapes=[
            pltpu.VMEM((64, 512, 128), F32),
            pltpu.VMEM((8, 1024, 1024), BF16),
            pltpu.VMEM((4, 1024, 128), F32),
            pltpu.VMEM((4, 1024, 128), F32),
            pltpu.VMEM((512, 1024), BF16),
            pltpu.VMEM((512, 1024), BF16),
            pltpu.VMEM((512, 1024), BF16),
            pltpu.VMEM((2, 512, 512), BF16),
            pltpu.VMEM((2, 512, 512), BF16),
            pltpu.VMEM((2, 256, 256), BF16),
            pltpu.VMEM((2, 256, 256), BF16),
            pltpu.VMEM((128, 128), F32),
            pltpu.VMEM((2, 6, 4, 128, 128), F32),
            pltpu.VMEM((3, 6, 4, 128, 128), F32),
            pltpu.VMEM((8, 128, 128), F32),
            pltpu.VMEM((3, 128, 1024), F32),
            pltpu.VMEM((3, 128, 1024), F32),
            pltpu.VMEM((384, 1024), BF16),
            pltpu.VMEM((8, 4, 64, 128), F32),
            dma((2, 3)), dma((6,)), dma((8,)), dma((2,)), dma((4,)),
            dma, dma, dma((4,)), dma((4,)),
            dma((5,)), dma((5, 3)), dma((2,)), dma((4,)),
            dma((8,)), dma((8,)), dma((8,)), dma((8, 2)), dma((8,)), dma((8,)),
        ],
        compiler_params=pltpu.CompilerParams(
            collective_id=0, has_side_effects=True, vmem_limit_bytes=62 << 20
        ),
    )(
        skip_gain.reshape(1, -1), inner_gate, signal, filter_taps, outer_gate, out_weight, *tables(),
    )
    return projected


def solution(mesh):
    in_specs = (
        P("ctx", "tp"),
        P("ctx", "tp"),
        P("ctx", "tp"),
        P("ctx", "tp"),
        P("tp"),
        P("tp", None),
    )
    return jax.shard_map(shards, mesh=mesh, in_specs=in_specs, out_specs=P("ctx", "tp"), check_vma=False)
```
